32 devices in a mesh: strip: 8 (over z, x), frames: 4 (over y, core).
Axes of the slice: x: 2, y: 2, z: 4, core: 2. Of those that a mesh axis runs over, the one named last changes fastest.
Arguments:
- frames: float32 [32, 512, 512], P('frames', 'strip'), may hold values from -6 to 6
- kernel: float32 [2, 512, 512], P(None, 'frames', 'strip'), may hold values from -6 to 6
- owner_rank: int32 [4, 8], P('frames'), may hold values from 0 to 7, each once within a row
- block_ids: int32 [32, 16], P('frames'), may hold values from 0 to 63
- block_counts: int32 [32], P('frames'), may hold values from 1 to 16, 256 in all
Outputs:
- disk_blocks: float32 [8, 64, 4096], P('strip', 'frames')
The draws below stay inside these ranges and needn't reach their ends.
Inputs may be any that keep to these rules, and one draw needn't show every extreme that they name: `owner_rank`: each row lists every rank of a group once; owner s of a group owns the one frame of rank s. `block_ids`: slots at or beyond a frame's count are unused. `block_counts`: some frame uses all 16 slots.
All inputs are finite; a program needn't handle non-finite values. No bound on the sum of `block_counts` on one device may be relied on, other than what follows from the above.
Results may differ from the reference program's by a relative error of at most 0.0003.
Values sent between devices are 32-bit elements; how exact they have to be, the bound alone decides.
No kernel may reach another device: no remote copies, remote signals or barrier semaphores. Data moves between devices by JAX's collectives and lax.ppermute only.
A program may use at most 64 MiB of HBM per device.

```python
import math
import jax
import jax.numpy as jnp
import numpy as np
from jax import lax

DET = 512
BLK = 64
NB = 8
MAXB = 16
FPO = 1
FR_LOC = 8
FRAMES = 32
N_STRIP = 8
N_FRAMES = 4


def plant(entries, own_key, smallest, top_value):
    longest = entries.shape.index(max(entries.shape))
    spots = []
    for shift in (0, 1):
        where = [jax.random.randint(jax.random.fold_in(own_key, axis), (), 0, length) for axis, length in enumerate(entries.shape)]
        where[longest] = (where[longest] + shift) % entries.shape[longest]
        spots.append(tuple(where))
    return entries.at[spots[0]].set(smallest).at[spots[1]].set(top_value)


def shard_levels(rng, dims, pieces, low, largest):
    def one(dim, parts):
        steps = jax.random.uniform(jax.random.fold_in(jax.random.fold_in(rng, 6), dim), (parts,), jnp.float32, low / len(pieces), largest / len(pieces))
        return jnp.repeat(jnp.exp(steps), dims[dim] // parts).reshape((-1,) + (1,) * (len(dims) - dim - 1))

    factor_of = one(*pieces[0])
    for cut in pieces[1:]:
        factor_of = factor_of * one(*cut)
    return factor_of


def split_up(amount, total, reach, slope):
    portions = [(1 << 20) // math.isqrt(standing ** slope) + 1 for standing in range(2, amount + 1)]
    spare, counts = total - reach - (amount - 1), [1] * (amount - 1)
    while spare > 0:
        candidates = [i for i in range(amount - 1) if counts[i] < reach]
        pool, left = sum([portions[i] for i in candidates]), spare
        for i in candidates:
            addition = min(reach - counts[i], max(1, left * portions[i] // pool), spare)
            counts[i] = counts[i] + addition
            spare = spare - addition
    return np.array([reach] + counts)


def ragged(key, number_of, total, most, skew):
    if number_of == 2:
        one = jax.random.randint(key, (), max(1, total - most), min(most, total - 1) + 1)
        return jnp.stack([one, total - one])
    sizes = jnp.asarray(split_up(number_of, total, most, skew), jnp.int32)
    couples = (number_of - 1) // 2
    source_of, receiver = sizes[1:1 + 2 * couples:2], sizes[2:2 + 2 * couples:2]
    room = jnp.minimum(source_of - 1, most - receiver)
    shifted = jax.random.randint(jax.random.fold_in(key, 1), (couples,), 0, 1 << 20) % (room + 1)
    sizes = sizes.at[1:1 + 2 * couples:2].set(source_of - shifted).at[2:2 + 2 * couples:2].set(receiver + shifted)
    return sizes[jax.random.permutation(jax.random.fold_in(key, 2), number_of)]


def scatter_about(stream_key, dims, spread, most, pieces=(), kind=jnp.bfloat16):
    drawn = spread * jax.random.normal(stream_key, dims, jnp.float32)
    if pieces:
        drawn = drawn * shard_levels(stream_key, dims, pieces, -0.22, 0.18)
    return jnp.clip(drawn, -most, most).astype(kind)


def setup_inputs(seed: int = 0) -> dict:
    splits = jax.random.split(jax.random.key(seed), 6)
    frames = scatter_about(splits[0], (FRAMES, DET, DET), 1.0, 6.0, ((0, 4), (1, 8)), jnp.float32)
    kernel = scatter_about(splits[1], (2, DET, DET), 1.0, 6.0, ((1, 4), (2, 8)), jnp.float32)
    owner_rank = jax.vmap(lambda own: jax.random.permutation(own, FR_LOC))(jax.random.split(splits[2], N_FRAMES)).reshape((N_FRAMES, FR_LOC)).astype(jnp.int32)
    block_ids = plant(jax.random.randint(splits[3], (FRAMES, MAXB), 0, NB * NB), jax.random.fold_in(splits[3], 1), 0, (NB * NB) - 1).astype(jnp.int32)
    block_counts = ragged(splits[4], FRAMES, FRAMES * MAXB // 2, MAXB, 0).astype(jnp.int32)
    return {"frames": frames, "kernel": kernel, "owner_rank": owner_rank, "block_ids": block_ids, "block_counts": block_counts}


def corr_frame(frame, kernel_c):
    spectrum = jnp.fft.fft2(frame) * kernel_c
    return jnp.real(jnp.fft.ifft2(spectrum))


def reference(frames, kernel, owner_rank, block_ids, block_counts):
    kernel_c = kernel[0] + 1j * kernel[1]

    def frame_blocks(items):
        frame, frame_ids, frame_count = items
        correlation = corr_frame(frame, kernel_c)
        tile_rows = correlation.reshape(NB, BLK, NB, BLK).transpose(0, 2, 1, 3).reshape(NB * NB, BLK * BLK)
        picked = tile_rows[frame_ids]
        keep_mask = jnp.arange(MAXB, dtype=jnp.int32) < frame_count
        return jnp.where(keep_mask[:, None], picked, jnp.zeros_like(picked))

    per_frame = lax.map(frame_blocks, (frames, block_ids, block_counts))
    rank_list = owner_rank.reshape(-1)
    group_index = jnp.arange(N_FRAMES * FR_LOC, dtype=jnp.int32) // FR_LOC
    destination = (rank_list // FPO) * (N_FRAMES * FPO) + group_index * FPO + rank_list % FPO
    collected = jnp.zeros((N_STRIP * N_FRAMES * FPO, MAXB, BLK * BLK), per_frame.dtype).at[destination].set(per_frame)
    return collected.reshape(N_STRIP, N_FRAMES * FPO * MAXB, BLK * BLK)
```

```python
import functools

import jax
import jax.numpy as jnp
import numpy as np
from jax import lax
from jax.experimental import pallas as pl
from jax.experimental.pallas import tpu as pltpu
from jax.sharding import PartitionSpec as P

BLK = 64
NB = 8
MAXB = 16

VMEM = pltpu.VMEM
SMEM = pltpu.SMEM
BF16 = jnp.bfloat16
HEAPCOST = 1024
PACKCOST = 1024
F32 = jnp.float32


def halves(table):
    high = table.astype(np.float32).astype(jnp.bfloat16)
    low = (table - high.astype(np.float64)).astype(np.float32).astype(jnp.bfloat16)
    return np.stack([high, low])


@functools.cache
def tables(detector):
    half = detector // 2
    quarter = detector // 4
    turn = 2.0 * np.pi / detector
    place = np.arange(half)

    def wave(freqs, function):
        return function(turn * (np.outer(place, freqs) % detector))

    even_v = 2 * np.arange(quarter)
    odd_v = even_v + 1
    even_im = -wave(even_v, np.sin)
    even_im[:, 0] = np.where(place % 2 == 0, 1.0, -1.0)
    row_even = np.concatenate([wave(even_v, np.cos), even_im], axis=1)
    row_odd = np.concatenate([wave(odd_v, np.cos), -wave(odd_v, np.sin)], axis=1)
    row = np.stack([row_even, row_odd])

    even_u = 2 * np.arange(half)
    cols = []
    invs = []
    order = place.reshape(half // BLK, BLK // 2, 2).transpose(0, 2, 1).reshape(-1)
    for freqs in (even_u, even_u + 1):
        cos, sin = wave(freqs, np.cos), wave(freqs, np.sin)
        cols.append(np.concatenate([cos.T, sin.T], axis=0))
        invs.append(np.concatenate([cos[order], sin[order]], axis=1))
    fin = np.stack([row_even.T, row_odd.T]) / (detector * detector)

    keep = np.zeros((half, half))
    flip = np.zeros((half, half))
    for slot, freq in enumerate(np.concatenate([even_v, odd_v])):
        keep[freq, slot] = 1.0
        flip[(half - freq) % half, slot] = 1.0
    perm = np.stack([keep, flip]).astype(jnp.bfloat16)
    return halves(row), halves(np.stack(cols)), halves(np.stack(invs)), halves(fin), perm


def split(value):
    high = value.astype(BF16)
    return high, (value - high.astype(F32)).astype(BF16)


def dot(left, right):
    return jnp.dot(left, right, preferred_element_type=F32)


def dot3(left, right):
    return dot(left[0], right[0]) + dot(left[1], right[0]) + dot(left[0], right[1])


def pack_kernel(count, rank_ref, frames_ref, *rest):
    outs, sems = rest[:count], rest[count]
    me = lax.axis_index("strip")
    copies = []
    for j in range(count):
        target = me ^ j
        source = jnp.int32(0)
        for i in range(count):
            source = source + jnp.where(rank_ref[0, i] == target, i, 0)
        copies.append(pltpu.make_async_copy(frames_ref.at[source], outs[j], sems.at[j]))
        copies[-1].start()
    for copy in copies:
        copy.wait()


def pack(owner_rank, frames):
    count, rows, detector = frames.shape
    return pl.pallas_call(
        functools.partial(pack_kernel, count),
        out_shape=[jax.ShapeDtypeStruct((rows, detector), F32)] * count,
        in_specs=[pl.BlockSpec(memory_space=SMEM), pl.BlockSpec(memory_space=pl.ANY)],
        out_specs=[pl.BlockSpec(memory_space=VMEM)] * count,
        scratch_shapes=[pltpu.SemaphoreType.DMA((count,))],
        compiler_params=pltpu.CompilerParams(vmem_limit_bytes=60 << 20),
        cost_estimate=pl.CostEstimate(flops=PACKCOST, bytes_accessed=1024, transcendentals=0),
        name="pack",
    )(owner_rank, frames)


def heap_kernel(*refs):
    for i, ref in enumerate(refs[:-1]):
        refs[-1][i] = ref[...]


def heap(parts):
    return pl.pallas_call(
        heap_kernel,
        out_shape=jax.ShapeDtypeStruct((len(parts),) + parts[0].shape, F32),
        in_specs=[pl.BlockSpec(memory_space=VMEM)] * len(parts),
        out_specs=pl.BlockSpec(memory_space=VMEM),
        compiler_params=pltpu.CompilerParams(vmem_limit_bytes=8 << 20),
        cost_estimate=pl.CostEstimate(flops=HEAPCOST, bytes_accessed=1024, transcendentals=0),
        name="heap",
    )(*parts)


def turned(left, right):
    return lax.dot_general(left, right, (((0,), (0,)), ((), ())), preferred_element_type=F32)


def fold_tiles(scr, perm_ref, out_ref):
    half = perm_ref.shape[1]
    lane = lax.broadcasted_iota(jnp.int32, (128, 128), 1)
    for part in range(2):
        for tile in range(scr.shape[1]):
            left, right = split(scr[part, tile, 0:half]), split(scr[part, tile, half:])
            plus = turned(left[0], perm_ref[0]) + turned(left[1], perm_ref[0])
            minus = turned(right[0], perm_ref[1]) + turned(right[1], perm_ref[1])
            for group in range(2):
                p, m = (x[:, group * 128 : (group + 1) * 128] for x in (plus, minus))
                both, diff = p + m, p - m
                if group == 0:
                    both, diff = jnp.where(lane == 0, p, both), jnp.where(lane == 0, m, diff)
                out_ref[part, group, tile * 128 : (tile + 1) * 128] = both
                out_ref[2 + part, group, tile * 128 : (tile + 1) * 128] = diff


def fold_pieces_kernel(*refs):
    quads, perm_ref, out_ref, scr = refs[:8], refs[8], refs[9], refs[10]
    strip, group = lax.axis_index("strip"), lax.axis_index("frames")
    for df in range(4):
        for dx in range(2):
            for j in range(4):
                base = pl.multiple_of((strip ^ (2 * j + dx)) * BLK, BLK)
                for part in range(2):
                    scr[part, group ^ df, pl.ds(base, BLK)] = quads[2 * df + dx][j, part]
    fold_tiles(scr, perm_ref, out_ref)


def fold_whole_kernel(kern_ref, perm_ref, out_ref, scr):
    for part in range(2):
        for tile in range(scr.shape[1]):
            scr[part, tile] = kern_ref[part, :, tile * 128 : (tile + 1) * 128]
    fold_tiles(scr, perm_ref, out_ref)


def fold(body, args, perm, detector):
    return pl.pallas_call(
        body,
        out_shape=jax.ShapeDtypeStruct((4, 2, detector, detector // 4), F32),
        in_specs=[pl.BlockSpec(memory_space=VMEM)] * (len(args) + 1),
        out_specs=pl.BlockSpec(memory_space=VMEM),
        scratch_shapes=[VMEM((2, detector // 128, detector, 128), F32)],
        compiler_params=pltpu.CompilerParams(vmem_limit_bytes=32 << 20),
        cost_estimate=pl.CostEstimate(flops=1024, bytes_accessed=1024, transcendentals=0),
        name="fold",
    )(*args, perm)


def correlate_kernel(pieces, *refs):
    rank_ref, ids_ref, counts_ref = refs[:3]
    strips = refs[3 : 3 + pieces]
    fold_ref, row_ref, col_ref, inv_ref, fin_ref, out_ref, sums, img, blocks = refs[3 + pieces :]
    detector = fold_ref.shape[2]
    half, quarter = detector // 2, detector // 4
    me = lax.axis_index("strip")

    if pieces == 1:
        sums[0:half] = strips[0][0:half] + strips[0][half:]
        sums[half:] = strips[0][0:half] - strips[0][half:]
    else:
        rows = detector // pieces
        sign = jnp.where(me >= pieces // 2, -1.0, 1.0).astype(F32)
        for j in range(pieces // 2):
            base = pl.multiple_of(((me ^ j) % (pieces // 2)) * rows, rows)
            one, two = strips[j][...], strips[j + pieces // 2][...]
            sums[pl.ds(base, rows)] = one + two
            sums[pl.ds(base + half, rows)] = (one - two) * sign

    left, right = sums[:, 0:half], sums[:, half:]
    spec_even = split(dot3(split(left + right), (row_ref[0, 0], row_ref[1, 0])))
    spec_odd = split(dot3(split(left - right), (row_ref[0, 1], row_ref[1, 1])))

    lane = lax.broadcasted_iota(jnp.int32, (half, quarter), 1)
    back = []
    for parity in range(2):
        table = (col_ref[0, parity], col_ref[1, parity])
        where = slice(parity * half, (parity + 1) * half)
        parts = []
        for group, spec in enumerate((spec_even, spec_odd)):
            both = dot3(table, (spec[0][where], spec[1][where]))
            cos_re, cos_im = both[0:half, 0:quarter], both[0:half, quarter:]
            sin_re, sin_im = both[half:, 0:quarter], both[half:, quarter:]
            freqs = pl.ds(parity, half, stride=2)
            sum_re, sum_im = fold_ref[0, group, freqs, :], fold_ref[1, group, freqs, :]
            dif_re, dif_im = fold_ref[2, group, freqs, :], fold_ref[3, group, freqs, :]
            two_re, two_im = sum_re, sum_im
            if group == 0:
                two_re, two_im = jnp.where(lane == 0, dif_re, sum_re), jnp.where(lane == 0, dif_im, sum_im)
                dif_re, dif_im = jnp.where(lane == 0, 0.0, dif_re), jnp.where(lane == 0, 0.0, dif_im)
            plus_re = cos_re * sum_re + sin_im * dif_re - cos_im * dif_im + sin_re * sum_im
            plus_im = cos_re * sum_im + sin_im * dif_im + cos_im * dif_re - sin_re * sum_re
            minus_re = cos_re * dif_re + sin_im * two_re - cos_im * two_im + sin_re * dif_im
            minus_im = cos_re * dif_im + sin_im * two_im + cos_im * two_re - sin_re * dif_re
            upper = split(jnp.concatenate([plus_re, minus_im], axis=1))
            lower = split(jnp.concatenate([-plus_im, minus_re], axis=1))
            parts.append([jnp.concatenate([u, w], axis=0) for u, w in zip(upper, lower)])
        table = (inv_ref[0, parity], inv_ref[1, parity])
        back.append([dot3(table, part) for part in parts])

    for upper in range(2):
        ends = []
        for group in range(2):
            even, odd = back[0][group], back[1][group]
            rows = split(even - odd if upper else even + odd)
            ends.append(dot3(rows, (fin_ref[0, group], fin_ref[1, group])))
        where = slice(upper * half, (upper + 1) * half)
        for side, value in enumerate((ends[0] + ends[1], ends[0] - ends[1])):
            for t in range(half // 128):
                img[side * (half // 128) + t, where] = value[:, t * 128 : (t + 1) * 128]

    own = jnp.int32(0)
    for i in range(rank_ref.shape[1]):
        own = own + jnp.where(rank_ref[0, i] == me, i, 0)
    used = counts_ref[own]
    pairs = BLK // 2
    lane = lax.broadcasted_iota(jnp.int32, (pairs, 2 * BLK), 1)
    for m in range(MAXB):
        block = jnp.clip(ids_ref[own, m], 0, NB * NB - 1)
        base = pl.multiple_of((block // NB) * BLK, BLK)
        tile = (block % NB) // 2
        even = img[tile, pl.ds(base, pairs)]
        odd = img[tile, pl.ds(base + pairs, pairs)]
        second = jnp.broadcast_to(block % 2 == 1, lane.shape)
        value = jnp.where(
            lane < BLK,
            jnp.where(second, pltpu.roll(even, BLK, 1), even),
            jnp.where(second, odd, pltpu.roll(odd, BLK, 1)),
        )
        blocks[m * pairs : (m + 1) * pairs] = jnp.where(m < used, value, 0.0)
    for j in range(pairs):
        out_ref[0, :, j * 2 * BLK : (j + 1) * 2 * BLK] = blocks[pl.ds(j, MAXB, stride=pairs), :]


def correlate(owner_rank, block_ids, block_counts, strips, folded, consts):
    detector = folded.shape[2]
    half = detector // 2
    return pl.pallas_call(
        functools.partial(correlate_kernel, len(strips)),
        out_shape=jax.ShapeDtypeStruct((1, MAXB, BLK * BLK), F32),
        in_specs=[pl.BlockSpec(memory_space=SMEM)] * 3
        + [pl.BlockSpec(memory_space=VMEM)] * (len(strips) + 1 + len(consts)),
        out_specs=pl.BlockSpec(memory_space=VMEM),
        scratch_shapes=[
            VMEM((detector, detector), F32),
            VMEM((detector // 128, detector, 128), F32),
            VMEM((MAXB * BLK // 2, 2 * BLK), F32),
        ],
        compiler_params=pltpu.CompilerParams(vmem_limit_bytes=40 << 20),
        name="correlate",
    )(owner_rank, block_ids, block_counts, *strips, folded, *consts)


def swap(value, axis, size, bits):
    return lax.ppermute(value, axis, [(i, i ^ bits) for i in range(size)])


def shards(strip_size, group_size, frames, kernel, owner_rank, block_ids, block_counts):
    detector = frames.shape[2]
    *consts, perm = tables(detector)
    if strip_size == 8 and group_size == 4:
        tie = lax.optimization_barrier
        blocks = list(pack(owner_rank, frames))
        strips = {0: blocks[0]}
        piece = jnp.swapaxes(kernel, 1, 2)
        far = swap(piece, "strip", 8, 4)
        near = swap(piece, "strip", 8, 2)
        both = swap(far, "strip", 8, 2)
        for j in (4, 6, 1):
            strips[j] = swap(blocks[j], "strip", 8, j)
        near, far, both, strips[4], strips[1], blocks[5], blocks[7], blocks[2], blocks[3] = tie((near, far, both, strips[4], strips[1], blocks[5], blocks[7], blocks[2], blocks[3]))
        quad = heap([piece, near, far, both])
        quad_x = swap(quad, "strip", 8, 1)
        quad, strips[6] = tie((quad, strips[6]))
        quad_y = swap(quad, "frames", 4, 2)
        for j in (5, 7, 2, 3):
            strips[j] = swap(blocks[j], "strip", 8, j)
        quad_x, strips[5], strips[2] = tie((quad_x, strips[5], strips[2]))
        quad_xy = swap(quad_x, "frames", 4, 2)
        quads = [quad, quad_x, quad_y, quad_xy]
        *quads, strips[7], strips[3] = tie((*quads, strips[7], strips[3]))
        quads = quads + [swap(q, "frames", 4, 1) for q in quads]
        ordered = [quads[4 * (df % 2) + 2 * (df // 2) + dx] for df in range(4) for dx in range(2)]
        folded = fold(fold_pieces_kernel, ordered, perm, detector)
        strips = [strips[j] for j in range(8)]
    else:
        places = jnp.argsort(owner_rank.reshape(-1))
        strips = [lax.all_to_all(frames[places], "strip", split_axis=0, concat_axis=1, tiled=True)[0]]
        whole = lax.all_gather(kernel, "strip", axis=2, tiled=True)
        whole = lax.all_gather(whole, "frames", axis=1, tiled=True)
        folded = fold(fold_whole_kernel, [jnp.swapaxes(whole, 1, 2)], perm, detector)
    return correlate(owner_rank, block_ids, block_counts, strips, folded, consts)


def solution(mesh):
    return jax.shard_map(
        functools.partial(shards, mesh.shape["strip"], mesh.shape["frames"]),
        mesh=mesh,
        in_specs=(
            P("frames", "strip", None),
            P(None, "frames", "strip"),
            P("frames", None),
            P("frames", None),
            P("frames"),
        ),
        out_specs=P("strip", "frames", None),
        check_vma=False,
    )
```

```python
import functools

import jax
import jax.numpy as jnp
import numpy as np
from jax import lax
from jax.experimental import pallas as pl
from jax.experimental.pallas import tpu as pltpu
from jax.sharding import PartitionSpec as P

BLK = 64
NB = 8
MAXB = 16

VMEM = pltpu.VMEM
SMEM = pltpu.SMEM
BF16 = jnp.bfloat16
XLAST = False
ZDIRECT = 0
HEAPCOST = 500000000
PACKCOST = 2000000000
FOLDCOST = 3000000000
EDGES = [['ky', 'f5'], ['heap', 'r0'], ['kx', 'kc0'], ['pack', 'kc1']]
COSTS = [4000000000, 6000000000, 2000000000, 1500000000]
OPS = [('pack', []), ('far', []), ('near', []), ('both', ['far']), ('heap', ['near', 'far', 'both']), ('kx', ['heap']), ('ky', ['heap']), ('kxy', ['kx']), ('kc0', ['heap']), ('kc1', ['kx']), ('kc2', ['ky']), ('kc3', ['kxy']), ('f1', ['pack']), ('f2', ['pack']), ('f3', ['pack']), ('f4', ['pack']), ('f5', ['pack']), ('f6', ['pack']), ('f7', ['pack']), ('r0', ['pack', 'f4']), ('r1', ['f1', 'f5']), ('r2', ['f2', 'f6']), ('r3', ['f3', 'f7'])]
ROWCOST = 1024
F32 = jnp.float32


def halves(table):
    high = table.astype(np.float32).astype(jnp.bfloat16)
    low = (table - high.astype(np.float64)).astype(np.float32).astype(jnp.bfloat16)
    return np.stack([high, low])


@functools.cache
def tables(detector):
    half = detector // 2
    quarter = detector // 4
    turn = 2.0 * np.pi / detector
    place = np.arange(half)

    def wave(freqs, function):
        return function(turn * (np.outer(place, freqs) % detector))

    even_v = 2 * np.arange(quarter)
    odd_v = even_v + 1
    even_im = -wave(even_v, np.sin)
    even_im[:, 0] = np.where(place % 2 == 0, 1.0, -1.0)
    row_even = np.concatenate([wave(even_v, np.cos), even_im], axis=1)
    row_odd = np.concatenate([wave(odd_v, np.cos), -wave(odd_v, np.sin)], axis=1)
    row = np.stack([row_even, row_odd])

    even_u = 2 * np.arange(half)
    cols = []
    invs = []
    order = place.reshape(half // BLK, BLK // 2, 2).transpose(0, 2, 1).reshape(-1)
    for freqs in (even_u, even_u + 1):
        cos, sin = wave(freqs, np.cos), wave(freqs, np.sin)
        cols.append(np.concatenate([cos.T, sin.T], axis=0))
        invs.append(np.concatenate([cos[order], sin[order]], axis=1))
    fin = np.stack([row_even.T, row_odd.T]) / (detector * detector)

    keep = np.zeros((half, half))
    flip = np.zeros((half, half))
    for slot, freq in enumerate(np.concatenate([even_v, odd_v])):
        keep[freq, slot] = 1.0
        flip[(half - freq) % half, slot] = 1.0
    perm = np.stack([keep, flip]).astype(jnp.bfloat16)
    return halves(row), halves(np.stack(cols)), halves(np.stack(invs)), halves(fin), perm


def split(value):
    high = value.astype(BF16)
    return high, (value - high.astype(F32)).astype(BF16)


def dot(left, right):
    return jnp.dot(left, right, preferred_element_type=F32)


def dot3(left, right):
    return dot(left[0], right[0]) + dot(left[1], right[0]) + dot(left[0], right[1])


def pack_kernel(rank_ref, frames_ref, *outs):
    me = lax.axis_index("strip")
    ranks = rank_ref[...]
    places = lax.broadcasted_iota(jnp.int32, ranks.shape, 1)
    for j, out in enumerate(outs):
        out[...] = frames_ref[jnp.sum(jnp.where(ranks == (me ^ j), places, 0))]


def pack(owner_rank, frames):
    count, rows, detector = frames.shape
    return pl.pallas_call(
        pack_kernel,
        out_shape=[jax.ShapeDtypeStruct((rows, detector), F32)] * count,
        in_specs=[pl.BlockSpec(memory_space=VMEM)] * 2,
        out_specs=[pl.BlockSpec(memory_space=VMEM)] * count,
        compiler_params=pltpu.CompilerParams(vmem_limit_bytes=16 << 20),
        cost_estimate=pl.CostEstimate(flops=PACKCOST, bytes_accessed=1024, transcendentals=0),
        name="pack",
    )(owner_rank, frames)


def heap_kernel(*refs):
    for i, ref in enumerate(refs[:-1]):
        refs[-1][i] = ref[...]


def heap(parts):
    return pl.pallas_call(
        heap_kernel,
        out_shape=jax.ShapeDtypeStruct((len(parts),) + parts[0].shape, F32),
        in_specs=[pl.BlockSpec(memory_space=VMEM)] * len(parts),
        out_specs=pl.BlockSpec(memory_space=VMEM),
        compiler_params=pltpu.CompilerParams(vmem_limit_bytes=8 << 20),
        cost_estimate=pl.CostEstimate(flops=HEAPCOST, bytes_accessed=1024, transcendentals=0),
        name="heap",
    )(*parts)


def turned(left, right):
    return lax.dot_general(left, right, (((0,), (0,)), ((), ())), preferred_element_type=F32)


def fold_tiles(scr, perm_ref, out_ref):
    half = perm_ref.shape[1]
    lane = lax.broadcasted_iota(jnp.int32, (128, 128), 1)
    for part in range(2):
        for tile in range(scr.shape[1]):
            left, right = split(scr[part, tile, 0:half]), split(scr[part, tile, half:])
            plus = turned(left[0], perm_ref[0]) + turned(left[1], perm_ref[0])
            minus = turned(right[0], perm_ref[1]) + turned(right[1], perm_ref[1])
            for group in range(2):
                p, m = (x[:, group * 128 : (group + 1) * 128] for x in (plus, minus))
                both, diff = p + m, p - m
                if group == 0:
                    both, diff = jnp.where(lane == 0, p, both), jnp.where(lane == 0, m, diff)
                out_ref[part, group, tile * 128 : (tile + 1) * 128] = both
                out_ref[2 + part, group, tile * 128 : (tile + 1) * 128] = diff


def fold_pieces_kernel(*refs):
    quads, perm_ref, out_ref, scr = refs[:8], refs[8], refs[9], refs[10]
    strip, group = lax.axis_index("strip"), lax.axis_index("frames")
    for df in range(4):
        for dx in range(2):
            for j in range(4):
                base = pl.multiple_of((strip ^ (2 * j + dx)) * BLK, BLK)
                for part in range(2):
                    scr[part, group ^ df, pl.ds(base, BLK)] = quads[2 * df + dx][j, part]
    fold_tiles(scr, perm_ref, out_ref)


def fold_whole_kernel(kern_ref, perm_ref, out_ref, scr):
    for part in range(2):
        for tile in range(scr.shape[1]):
            scr[part, tile] = kern_ref[part, :, tile * 128 : (tile + 1) * 128]
    fold_tiles(scr, perm_ref, out_ref)


def fold(body, args, perm, detector):
    return pl.pallas_call(
        body,
        out_shape=jax.ShapeDtypeStruct((4, 2, detector, detector // 4), F32),
        in_specs=[pl.BlockSpec(memory_space=VMEM)] * (len(args) + 1),
        out_specs=pl.BlockSpec(memory_space=VMEM),
        scratch_shapes=[VMEM((2, detector // 128, detector, 128), F32)],
        compiler_params=pltpu.CompilerParams(vmem_limit_bytes=32 << 20),
        cost_estimate=pl.CostEstimate(flops=FOLDCOST, bytes_accessed=1024, transcendentals=0),
        name="fold",
    )(*args, perm)


def rows_kernel(split_strip, lower_ref, upper_ref, row_ref, *rest):
    out_ref = rest[-1]
    rows, half = lower_ref.shape[0], lower_ref.shape[1] // 2
    one, two = lower_ref[...], upper_ref[...]
    diff = one - two
    if split_strip:
        diff = jnp.where(lax.axis_index("strip") >= split_strip, -diff, diff)
    both = jnp.concatenate([one + two, diff], axis=0)
    left, right = both[:, 0:half], both[:, half:]
    for group, value in enumerate((left + right, left - right)):
        parts = split(dot3(split(value), (row_ref[0, group], row_ref[1, group])))
        for i, part in enumerate(parts):
            for parity in range(2):
                out_ref[i, parity, :, group * half : (group + 1) * half] = part[parity * rows : (parity + 1) * rows]


def row_spectra(lower, upper, table, split_strip, flops, before=()):
    rows, detector = lower.shape
    return pl.pallas_call(
        functools.partial(rows_kernel, split_strip),
        out_shape=jax.ShapeDtypeStruct((2, 2, rows, detector), BF16),
        in_specs=[pl.BlockSpec(memory_space=VMEM)] * 3 + [pl.BlockSpec(memory_space=pl.ANY)] * len(before),
        out_specs=pl.BlockSpec(memory_space=VMEM),
        compiler_params=pltpu.CompilerParams(vmem_limit_bytes=16 << 20),
        cost_estimate=pl.CostEstimate(flops=flops, bytes_accessed=1024, transcendentals=0),
        name="rows",
    )(lower, upper, table, *before)


def correlate_kernel(pieces, *refs):
    lists = refs[:3]
    spectra = refs[3 : 3 + pieces]
    fold_ref, col_ref, inv_ref, fin_ref, out_ref, spec, img, blocks, *scalars = refs[3 + pieces :]
    *scalars, sems = scalars
    copies = [pltpu.make_async_copy(x, y, sems.at[i]) for i, (x, y) in enumerate(zip(lists, scalars))]
    for copy in copies:
        copy.start()
    detector = fold_ref.shape[2]
    half, quarter = detector // 2, detector // 4
    me = lax.axis_index("strip")
    rows = half // pieces
    for j in range(pieces):
        base = pl.multiple_of(((me ^ j) % pieces) * rows, rows)
        spec[:, :, pl.ds(base, rows)] = spectra[j][...]

    lane = lax.broadcasted_iota(jnp.int32, (half, quarter), 1)
    back = []
    for parity in range(2):
        table = (col_ref[0, parity], col_ref[1, parity])
        parts = []
        for group in range(2):
            lanes = slice(group * half, (group + 1) * half)
            both = dot3(table, (spec[0, parity, :, lanes], spec[1, parity, :, lanes]))
            cos_re, cos_im = both[0:half, 0:quarter], both[0:half, quarter:]
            sin_re, sin_im = both[half:, 0:quarter], both[half:, quarter:]
            freqs = pl.ds(parity, half, stride=2)
            sum_re, sum_im = fold_ref[0, group, freqs, :], fold_ref[1, group, freqs, :]
            dif_re, dif_im = fold_ref[2, group, freqs, :], fold_ref[3, group, freqs, :]
            two_re, two_im = sum_re, sum_im
            if group == 0:
                two_re, two_im = jnp.where(lane == 0, dif_re, sum_re), jnp.where(lane == 0, dif_im, sum_im)
                dif_re, dif_im = jnp.where(lane == 0, 0.0, dif_re), jnp.where(lane == 0, 0.0, dif_im)
            plus_re = cos_re * sum_re + sin_im * dif_re - cos_im * dif_im + sin_re * sum_im
            plus_im = cos_re * sum_im + sin_im * dif_im + cos_im * dif_re - sin_re * sum_re
            minus_re = cos_re * dif_re + sin_im * two_re - cos_im * two_im + sin_re * dif_im
            minus_im = cos_re * dif_im + sin_im * two_im + cos_im * two_re - sin_re * dif_re
            upper = split(jnp.concatenate([plus_re, minus_im], axis=1))
            lower = split(jnp.concatenate([-plus_im, minus_re], axis=1))
            parts.append([jnp.concatenate([u, w], axis=0) for u, w in zip(upper, lower)])
        table = (inv_ref[0, parity], inv_ref[1, parity])
        back.append([dot3(table, part) for part in parts])

    for upper in range(2):
        ends = []
        for group in range(2):
            even, odd = back[0][group], back[1][group]
            rows = split(even - odd if upper else even + odd)
            ends.append(dot3(rows, (fin_ref[0, group], fin_ref[1, group])))
        where = slice(upper * half, (upper + 1) * half)
        for side, value in enumerate((ends[0] + ends[1], ends[0] - ends[1])):
            for t in range(half // 128):
                img[side * (half // 128) + t, where] = value[:, t * 128 : (t + 1) * 128]

    for copy in copies:
        copy.wait()
    rank_ref, ids_ref, counts_ref = scalars
    own = jnp.int32(0)
    for i in range(rank_ref.shape[1]):
        own = own + jnp.where(rank_ref[0, i] == me, i, 0)
    used = counts_ref[own]
    pairs = BLK // 2
    lane = lax.broadcasted_iota(jnp.int32, (pairs, 2 * BLK), 1)
    for m in range(MAXB):
        block = jnp.clip(ids_ref[own, m], 0, NB * NB - 1)
        base = pl.multiple_of((block // NB) * BLK, BLK)
        tile = (block % NB) // 2
        even = img[tile, pl.ds(base, pairs)]
        odd = img[tile, pl.ds(base + pairs, pairs)]
        second = jnp.broadcast_to(block % 2 == 1, lane.shape)
        value = jnp.where(
            lane < BLK,
            jnp.where(second, pltpu.roll(even, BLK, 1), even),
            jnp.where(second, odd, pltpu.roll(odd, BLK, 1)),
        )
        blocks[m * pairs : (m + 1) * pairs] = jnp.where(m < used, value, 0.0)
    for j in range(pairs):
        out_ref[0, :, j * 2 * BLK : (j + 1) * 2 * BLK] = blocks[pl.ds(j, MAXB, stride=pairs), :]


def correlate(owner_rank, block_ids, block_counts, spectra, folded, consts):
    detector = folded.shape[2]
    return pl.pallas_call(
        functools.partial(correlate_kernel, len(spectra)),
        out_shape=jax.ShapeDtypeStruct((1, MAXB, BLK * BLK), F32),
        in_specs=[pl.BlockSpec(memory_space=pl.ANY)] * 3
        + [pl.BlockSpec(memory_space=VMEM)] * (len(spectra) + 1 + len(consts)),
        out_specs=pl.BlockSpec(memory_space=VMEM),
        scratch_shapes=[
            VMEM((2, 2, detector // 2, detector), BF16),
            VMEM((detector // 128, detector, 128), F32),
            VMEM((MAXB * BLK // 2, 2 * BLK), F32),
            SMEM(owner_rank.shape, jnp.int32),
            SMEM(block_ids.shape, jnp.int32),
            SMEM(block_counts.shape, jnp.int32),
            pltpu.SemaphoreType.DMA((3,)),
        ],
        compiler_params=pltpu.CompilerParams(vmem_limit_bytes=40 << 20),
        name="correlate",
    )(owner_rank, block_ids, block_counts, *spectra, folded, *consts)


def swap(value, axis, size, bits):
    return lax.ppermute(value, axis, [(i, i ^ bits) for i in range(size)])


def shards(strip_size, group_size, frames, kernel, owner_rank, block_ids, block_counts):
    detector = frames.shape[2]
    row_table, *consts, perm = tables(detector)
    if strip_size == 8 and group_size == 4:
        piece = jnp.swapaxes(kernel, 1, 2)
        needs = dict(OPS)
        val, order = {}, []

        def visit(name):
            if name in val:
                return
            deps = needs[name] + [a for a, b in EDGES if b == name]
            for d in deps:
                visit(d)

            def tied(value):
                extra = [val[a] for a, b in EDGES if b == name]
                return lax.optimization_barrier((value, extra))[0] if extra else value

            natural = [val[d] for d in needs[name]]
            if name == "pack":
                val[name] = pack(tied(owner_rank), frames)
            elif name == "far":
                val[name] = swap(tied(piece), "strip", 8, 4)
            elif name == "near":
                val[name] = swap(tied(piece), "strip", 8, 2)
            elif name == "both":
                val[name] = swap(tied(natural[0] if natural else piece), "strip", 8, {0: 2, 1: 6, 2: 4}[ZDIRECT])
            elif name == "heap":
                val[name] = heap([piece] + tied(natural))
            elif name in ("kx", "kxy") and not (name == "kxy" and not XLAST):
                val[name] = swap(tied(natural[0]), "strip", 8, 1)
            elif name in ("ky", "kxy"):
                val[name] = swap(tied(natural[0]), "frames", 4, 2)
            elif name[:2] == "kc":
                val[name] = swap(tied(natural[0]), "frames", 4, 1)
            elif name[0] == "f":
                val[name] = swap(tied(natural[0][int(name[1])]), "strip", 8, int(name[1]))
            elif name[0] == "r":
                j = int(name[1])
                low = natural[0][0] if j == 0 else natural[0]
                low, high = tied((low, natural[-1]))
                val[name] = row_spectra(low, high, row_table, 4, COSTS[j])

        for name in needs:
            visit(name)
        quads = [val["heap"], val["kx"], val["ky"], val["kxy"]] + [val["kc%d" % i] for i in range(4)]
        ordered = [quads[4 * (df % 2) + 2 * (df // 2) + dx] for df in range(4) for dx in range(2)]
        folded = fold(fold_pieces_kernel, ordered, perm, detector)
        spectra = [val["r%d" % j] for j in range(4)]
    else:
        places = jnp.argsort(owner_rank.reshape(-1))
        frame = lax.all_to_all(frames[places], "strip", split_axis=0, concat_axis=1, tiled=True)[0]
        whole = lax.all_gather(kernel, "strip", axis=2, tiled=True)
        whole = lax.all_gather(whole, "frames", axis=1, tiled=True)
        folded = fold(fold_whole_kernel, [jnp.swapaxes(whole, 1, 2)], perm, detector)
        spectra = [row_spectra(frame[: detector // 2], frame[detector // 2 :], row_table, 0, ROWCOST)]
    return correlate(owner_rank, block_ids, block_counts, spectra, folded, consts)


def solution(mesh):
    return jax.shard_map(
        functools.partial(shards, mesh.shape["strip"], mesh.shape["frames"]),
        mesh=mesh,
        in_specs=(
            P("frames", "strip", None),
            P(None, "frames", "strip"),
            P("frames", None),
            P("frames", None),
            P("frames"),
        ),
        out_specs=P("strip", "frames", None),
        check_vma=False,
    )
```

```python
import functools

import jax
import jax.numpy as jnp
import numpy as np
from jax import lax
from jax.experimental import pallas as pl
from jax.experimental.pallas import tpu as pltpu
from jax.sharding import PartitionSpec as P

BLK = 64
NB = 8
MAXB = 16

VMEM = pltpu.VMEM
SMEM = pltpu.SMEM
BF16 = jnp.bfloat16
XLAST = False
ZDIRECT = 0
HEAPCOST = 500000000
PACKCOST = 2000000000
FOLDCOST = 3000000000
EDGES = [['ky', 'f5'], ['heap', 'r0'], ['kx', 'kc0'], ['pack', 'kc1']]
COSTS = [4000000000, 6000000000, 2000000000, 1500000000]
PREP = True
PREPCOST = 5000000000
TABLESAT = -1
OPS = [('prep', []), ('pack', ['prep']), ('far', []), ('near', []), ('both', ['far']), ('heap', ['near', 'far', 'both']), ('kx', ['heap']), ('ky', ['heap']), ('kxy', ['kx']), ('kc0', ['heap']), ('kc1', ['kx']), ('kc2', ['ky']), ('kc3', ['kxy']), ('f1', ['pack']), ('f2', ['pack']), ('f3', ['pack']), ('f4', ['pack']), ('f5', ['pack']), ('f6', ['pack']), ('f7', ['pack']), ('r0', ['pack', 'f4']), ('r1', ['f1', 'f5']), ('r2', ['f2', 'f6']), ('r3', ['f3', 'f7'])]
ROWCOST = 1024
F32 = jnp.float32


def halves(table):
    high = table.astype(np.float32).astype(jnp.bfloat16)
    low = (table - high.astype(np.float64)).astype(np.float32).astype(jnp.bfloat16)
    return np.stack([high, low])


@functools.cache
def tables(detector):
    half = detector // 2
    quarter = detector // 4
    turn = 2.0 * np.pi / detector
    place = np.arange(half)

    def wave(freqs, function):
        return function(turn * (np.outer(place, freqs) % detector))

    even_v = 2 * np.arange(quarter)
    odd_v = even_v + 1
    even_im = -wave(even_v, np.sin)
    even_im[:, 0] = np.where(place % 2 == 0, 1.0, -1.0)
    row_even = np.concatenate([wave(even_v, np.cos), even_im], axis=1)
    row_odd = np.concatenate([wave(odd_v, np.cos), -wave(odd_v, np.sin)], axis=1)
    row = np.stack([row_even, row_odd])

    even_u = 2 * np.arange(half)
    cols = []
    invs = []
    order = place.reshape(half // BLK, BLK // 2, 2).transpose(0, 2, 1).reshape(-1)
    for freqs in (even_u, even_u + 1):
        cos, sin = wave(freqs, np.cos), wave(freqs, np.sin)
        cols.append(np.concatenate([cos.T, sin.T], axis=0))
        invs.append(np.concatenate([cos[order], sin[order]], axis=1))
    fin = np.stack([row_even.T, row_odd.T]) / (detector * detector)

    keep = np.zeros((half, half))
    flip = np.zeros((half, half))
    for slot, freq in enumerate(np.concatenate([even_v, odd_v])):
        keep[freq, slot] = 1.0
        flip[(half - freq) % half, slot] = 1.0
    perm = np.stack([keep, flip]).astype(jnp.bfloat16)
    return halves(row), halves(np.stack(cols)), halves(np.stack(invs)), halves(fin), perm


def split(value):
    high = value.astype(BF16)
    return high, (value - high.astype(F32)).astype(BF16)


def dot(left, right):
    return jnp.dot(left, right, preferred_element_type=F32)


def dot3(left, right):
    return dot(left[0], right[0]) + dot(left[1], right[0]) + dot(left[0], right[1])


def prepare_kernel(rank_ref, out_ref):
    out_ref[...] = rank_ref[...]


def prepare(owner_rank):
    return pl.pallas_call(
        prepare_kernel,
        out_shape=jax.ShapeDtypeStruct(owner_rank.shape, jnp.int32),
        in_specs=[pl.BlockSpec(memory_space=VMEM)],
        out_specs=pl.BlockSpec(memory_space=VMEM),
        compiler_params=pltpu.CompilerParams(vmem_limit_bytes=16 << 20),
        cost_estimate=pl.CostEstimate(flops=PREPCOST, bytes_accessed=1024, transcendentals=0),
        name="prepare",
    )(owner_rank)


def pack_kernel(rank_ref, frames_ref, *outs):
    me = lax.axis_index("strip")
    ranks = rank_ref[...]
    places = lax.broadcasted_iota(jnp.int32, ranks.shape, 1)
    for j, out in enumerate(outs):
        out[...] = frames_ref[jnp.sum(jnp.where(ranks == (me ^ j), places, 0))]


def pack(owner_rank, frames):
    count, rows, detector = frames.shape
    return pl.pallas_call(
        pack_kernel,
        out_shape=[jax.ShapeDtypeStruct((rows, detector), F32)] * count,
        in_specs=[pl.BlockSpec(memory_space=VMEM)] * 2,
        out_specs=[pl.BlockSpec(memory_space=VMEM)] * count,
        compiler_params=pltpu.CompilerParams(vmem_limit_bytes=16 << 20),
        cost_estimate=pl.CostEstimate(flops=PACKCOST, bytes_accessed=1024, transcendentals=0),
        name="pack",
    )(owner_rank, frames)


def heap_kernel(*refs):
    for i, ref in enumerate(refs[:-1]):
        refs[-1][i] = ref[...]


def heap(parts):
    return pl.pallas_call(
        heap_kernel,
        out_shape=jax.ShapeDtypeStruct((len(parts),) + parts[0].shape, F32),
        in_specs=[pl.BlockSpec(memory_space=VMEM)] * len(parts),
        out_specs=pl.BlockSpec(memory_space=VMEM),
        compiler_params=pltpu.CompilerParams(vmem_limit_bytes=8 << 20),
        cost_estimate=pl.CostEstimate(flops=HEAPCOST, bytes_accessed=1024, transcendentals=0),
        name="heap",
    )(*parts)


def turned(left, right):
    return lax.dot_general(left, right, (((0,), (0,)), ((), ())), preferred_element_type=F32)


def fold_tiles(scr, perm_ref, out_ref):
    half = perm_ref.shape[1]
    for part in range(2):
        for tile in range(scr.shape[1]):
            left, right = split(scr[part, tile, 0:half]), split(scr[part, tile, half:])
            plus = turned(left[0], perm_ref[0]) + turned(left[1], perm_ref[0])
            minus = turned(right[0], perm_ref[1]) + turned(right[1], perm_ref[1])
            for group in range(2):
                lanes = slice(group * 128, (group + 1) * 128)
                out_ref[part, group, tile * 128 : (tile + 1) * 128] = plus[:, lanes]
                out_ref[2 + part, group, tile * 128 : (tile + 1) * 128] = minus[:, lanes]


def fold_pieces_kernel(*refs):
    quads, perm_ref, out_ref, scr = refs[:8], refs[8], refs[9], refs[10]
    strip, group = lax.axis_index("strip"), lax.axis_index("frames")
    for df in range(4):
        for dx in range(2):
            for j in range(4):
                base = pl.multiple_of((strip ^ (2 * j + dx)) * BLK, BLK)
                for part in range(2):
                    scr[part, group ^ df, pl.ds(base, BLK)] = quads[2 * df + dx][j, part]
    fold_tiles(scr, perm_ref, out_ref)


def fold_whole_kernel(kern_ref, perm_ref, out_ref, scr):
    for part in range(2):
        for tile in range(scr.shape[1]):
            scr[part, tile] = kern_ref[part, :, tile * 128 : (tile + 1) * 128]
    fold_tiles(scr, perm_ref, out_ref)


def rows_kernel(split_strip, lower_ref, upper_ref, row_ref, *rest):
    out_ref = rest[-1]
    rows, half = lower_ref.shape[0], lower_ref.shape[1] // 2
    one, two = lower_ref[...], upper_ref[...]
    diff = one - two
    if split_strip:
        diff = jnp.where(lax.axis_index("strip") >= split_strip, -diff, diff)
    both = jnp.concatenate([one + two, diff], axis=0)
    left, right = both[:, 0:half], both[:, half:]
    for group, value in enumerate((left + right, left - right)):
        parts = split(dot3(split(value), (row_ref[0, group], row_ref[1, group])))
        for i, part in enumerate(parts):
            for parity in range(2):
                out_ref[i, parity, :, group * half : (group + 1) * half] = part[parity * rows : (parity + 1) * rows]


def row_spectra(lower, upper, table, split_strip, flops, before=()):
    rows, detector = lower.shape
    return pl.pallas_call(
        functools.partial(rows_kernel, split_strip),
        out_shape=jax.ShapeDtypeStruct((2, 2, rows, detector), BF16),
        in_specs=[pl.BlockSpec(memory_space=VMEM)] * (3 + len(before)),
        out_specs=pl.BlockSpec(memory_space=VMEM),
        compiler_params=pltpu.CompilerParams(vmem_limit_bytes=16 << 20),
        cost_estimate=pl.CostEstimate(flops=flops, bytes_accessed=1024, transcendentals=0),
        name="rows",
    )(lower, upper, table, *before)


def correlate_kernel(pieces, fold_body, *refs):
    tables, lists, refs = refs[:3], refs[3:6], refs[6:]
    spectra, kern, perm_ref, out_ref = refs[:pieces], refs[pieces:-15], refs[-15], refs[-14]
    scr, fold_ref, spec, img, blocks, col_ref, inv_ref, fin_ref, *scalars, sems, list_sems = refs[-13:]
    loads = [pltpu.make_async_copy(x, y, sems.at[i]) for i, (x, y) in enumerate(zip(tables, (col_ref, inv_ref, fin_ref)))]
    copies = [pltpu.make_async_copy(x, y, list_sems.at[i]) for i, (x, y) in enumerate(zip(lists, scalars))]
    for copy in loads + copies:
        copy.start()
    fold_body(*kern, perm_ref, fold_ref, scr)
    detector = fold_ref.shape[2]
    half, quarter = detector // 2, detector // 4
    me = lax.axis_index("strip")
    rows = half // pieces
    for j in range(pieces):
        base = pl.multiple_of(((me ^ j) % pieces) * rows, rows)
        spec[:, :, pl.ds(base, rows)] = spectra[j][...]

    lane = lax.broadcasted_iota(jnp.int32, (half, quarter), 1)
    back = []
    loads[0].wait()
    loads[1].wait()
    for parity in range(2):
        table = (col_ref[0, parity], col_ref[1, parity])
        parts = []
        for group in range(2):
            lanes = slice(group * half, (group + 1) * half)
            both = dot3(table, (spec[0, parity, :, lanes], spec[1, parity, :, lanes]))
            cos_re, cos_im = both[0:half, 0:quarter], both[0:half, quarter:]
            sin_re, sin_im = both[half:, 0:quarter], both[half:, quarter:]
            freqs = pl.ds(parity, half, stride=2)
            up_re, up_im = fold_ref[0, group, freqs, :], fold_ref[1, group, freqs, :]
            dn_re, dn_im = fold_ref[2, group, freqs, :], fold_ref[3, group, freqs, :]
            a_re, a_im = cos_re + sin_im, cos_im - sin_re
            b_re, b_im = cos_re - sin_im, -cos_im - sin_re
            if group == 0:
                a_re, a_im = jnp.where(lane == 0, cos_re, a_re), jnp.where(lane == 0, -sin_re, a_im)
                b_re, b_im = jnp.where(lane == 0, cos_im, b_re), jnp.where(lane == 0, -sin_im, b_im)
            p_re, p_im = a_re * up_re - a_im * up_im, a_re * up_im + a_im * up_re
            q_re, q_im = b_re * dn_re - b_im * dn_im, b_re * dn_im + b_im * dn_re
            plus_re, minus_im = p_re + q_re, p_im - q_im
            less_im, minus_re = -p_im - q_im, p_re - q_re
            if group == 0:
                plus_re, minus_im = jnp.where(lane == 0, p_re, plus_re), jnp.where(lane == 0, q_re, minus_im)
                less_im, minus_re = jnp.where(lane == 0, -p_im, less_im), jnp.where(lane == 0, -q_im, minus_re)
            upper = split(jnp.concatenate([plus_re, minus_im], axis=1))
            lower = split(jnp.concatenate([less_im, minus_re], axis=1))
            parts.append([jnp.concatenate([u, w], axis=0) for u, w in zip(upper, lower)])
        table = (inv_ref[0, parity], inv_ref[1, parity])
        back.append([dot3(table, part) for part in parts])

    loads[2].wait()
    for upper in range(2):
        ends = []
        for group in range(2):
            even, odd = back[0][group], back[1][group]
            rows = split(even - odd if upper else even + odd)
            ends.append(dot3(rows, (fin_ref[0, group], fin_ref[1, group])))
        where = slice(upper * half, (upper + 1) * half)
        for side, value in enumerate((ends[0] + ends[1], ends[0] - ends[1])):
            for t in range(half // 128):
                img[side * (half // 128) + t, where] = value[:, t * 128 : (t + 1) * 128]

    for copy in copies:
        copy.wait()
    rank_ref, ids_ref, counts_ref = scalars
    own = jnp.int32(0)
    for i in range(rank_ref.shape[1]):
        own = own + jnp.where(rank_ref[0, i] == me, i, 0)
    used = counts_ref[own]
    pairs = BLK // 2
    lane = lax.broadcasted_iota(jnp.int32, (pairs, 2 * BLK), 1)
    for m in range(MAXB):
        block = jnp.clip(ids_ref[own, m], 0, NB * NB - 1)
        base = pl.multiple_of((block // NB) * BLK, BLK)
        tile = (block % NB) // 2
        even = img[tile, pl.ds(base, pairs)]
        odd = img[tile, pl.ds(base + pairs, pairs)]
        second = jnp.broadcast_to(block % 2 == 1, lane.shape)
        value = jnp.where(
            lane < BLK,
            jnp.where(second, pltpu.roll(even, BLK, 1), even),
            jnp.where(second, odd, pltpu.roll(odd, BLK, 1)),
        )
        blocks[m * pairs : (m + 1) * pairs] = jnp.where(m < used, value, 0.0)
    for j in range(pairs):
        out_ref[0, :, j * 2 * BLK : (j + 1) * 2 * BLK] = blocks[pl.ds(j, MAXB, stride=pairs), :]


def correlate(owner_rank, block_ids, block_counts, spectra, fold_body, kern, perm, consts):
    detector = spectra[0].shape[-1]
    half = detector // 2
    return pl.pallas_call(
        functools.partial(correlate_kernel, len(spectra), fold_body),
        out_shape=jax.ShapeDtypeStruct((1, MAXB, BLK * BLK), F32),
        in_specs=[pl.BlockSpec(memory_space=pl.ANY)] * 6
        + [pl.BlockSpec(memory_space=VMEM)] * (len(spectra) + len(kern) + 1),
        out_specs=pl.BlockSpec(memory_space=VMEM),
        scratch_shapes=[
            VMEM((2, detector // 128, detector, 128), F32),
            VMEM((4, 2, detector, detector // 4), F32),
            VMEM((2, 2, half, detector), BF16),
            VMEM((detector // 128, detector, 128), F32),
            VMEM((MAXB * BLK // 2, 2 * BLK), F32),
        ]
        + [VMEM(x.shape, BF16) for x in consts]
        + [SMEM(x.shape, jnp.int32) for x in (owner_rank, block_ids, block_counts)]
        + [pltpu.SemaphoreType.DMA((3,)), pltpu.SemaphoreType.DMA((3,))],
        compiler_params=pltpu.CompilerParams(vmem_limit_bytes=48 << 20),
        name="correlate",
    )(*consts, owner_rank, block_ids, block_counts, *spectra, *kern, perm)


def swap(value, axis, size, bits):
    return lax.ppermute(value, axis, [(i, i ^ bits) for i in range(size)])


def shards(strip_size, group_size, frames, kernel, owner_rank, block_ids, block_counts):
    detector = frames.shape[2]
    row_table, *consts, perm = tables(detector)
    if strip_size == 8 and group_size == 4:
        piece = jnp.swapaxes(kernel, 1, 2)
        needs = dict(OPS)
        val, order = {}, []

        def visit(name):
            if name in val:
                return
            deps = needs[name] + [a for a, b in EDGES if b == name]
            for d in deps:
                visit(d)

            def tied(value):
                extra = [val[a] for a, b in EDGES if b == name]
                return lax.optimization_barrier((value, extra))[0] if extra else value

            natural = [val[d] for d in needs[name]]
            if name == "pack":
                val[name] = pack(tied(natural[0] if natural else owner_rank), frames)
            elif name == "prep":
                val[name] = prepare(tied(owner_rank))
            elif name == "far":
                val[name] = swap(tied(piece), "strip", 8, 4)
            elif name == "near":
                val[name] = swap(tied(piece), "strip", 8, 2)
            elif name == "both":
                val[name] = swap(tied(natural[0] if natural else piece), "strip", 8, {0: 2, 1: 6, 2: 4}[ZDIRECT])
            elif name == "heap":
                val[name] = heap([piece] + tied(natural))
            elif name in ("kx", "kxy") and not (name == "kxy" and not XLAST):
                val[name] = swap(tied(natural[0]), "strip", 8, 1)
            elif name in ("ky", "kxy"):
                val[name] = swap(tied(natural[0]), "frames", 4, 2)
            elif name[:2] == "kc":
                val[name] = swap(tied(natural[0]), "frames", 4, 1)
            elif name[0] == "f":
                val[name] = swap(tied(natural[0][int(name[1])]), "strip", 8, int(name[1]))
            elif name[0] == "r":
                j = int(name[1])
                low = natural[0][0] if j == 0 else natural[0]
                low, high = tied((low, natural[-1]))
                val[name] = row_spectra(low, high, row_table, 4, COSTS[j], consts if TABLESAT == j else ())

        for name in needs:
            visit(name)
        quads = [val["heap"], val["kx"], val["ky"], val["kxy"]] + [val["kc%d" % i] for i in range(4)]
        kern = [quads[4 * (df % 2) + 2 * (df // 2) + dx] for df in range(4) for dx in range(2)]
        fold_body = fold_pieces_kernel
        spectra = [val["r%d" % j] for j in range(4)]
    else:
        places = jnp.argsort(owner_rank.reshape(-1))
        frame = lax.all_to_all(frames[places], "strip", split_axis=0, concat_axis=1, tiled=True)[0]
        whole = lax.all_gather(kernel, "strip", axis=2, tiled=True)
        whole = lax.all_gather(whole, "frames", axis=1, tiled=True)
        fold_body, kern = fold_whole_kernel, [jnp.swapaxes(whole, 1, 2)]
        spectra = [row_spectra(frame[: detector // 2], frame[detector // 2 :], row_table, 0, ROWCOST)]
    return correlate(owner_rank, block_ids, block_counts, spectra, fold_body, kern, perm, consts)


def solution(mesh):
    return jax.shard_map(
        functools.partial(shards, mesh.shape["strip"], mesh.shape["frames"]),
        mesh=mesh,
        in_specs=(
            P("frames", "strip", None),
            P(None, "frames", "strip"),
            P("frames", None),
            P("frames", None),
            P("frames"),
        ),
        out_specs=P("strip", "frames", None),
        check_vma=False,
    )
```

```python
import functools

import jax
import jax.numpy as jnp
import numpy as np
from jax import lax
from jax.experimental import pallas as pl
from jax.experimental.pallas import tpu as pltpu
from jax.sharding import PartitionSpec as P

BLK = 64
NB = 8
MAXB = 16

VMEM = pltpu.VMEM
SMEM = pltpu.SMEM
BF16 = jnp.bfloat16

LITTLE = 1024
PREPARE_COST = 5_000_000_000
PACK_COST = 2_000_000_000
ROW_COSTS = (4_000_000_000, 6_000_000_000, 2_000_000_000, 1_500_000_000)
F32 = jnp.float32


def halves(table):
    high = table.astype(np.float32).astype(jnp.bfloat16)
    low = (table - high.astype(np.float64)).astype(np.float32).astype(jnp.bfloat16)
    return np.stack([high, low])


@functools.cache
def tables(detector):
    half = detector // 2
    quarter = detector // 4
    turn = 2.0 * np.pi / detector
    place = np.arange(half)

    def wave(freqs, function):
        return function(turn * (np.outer(place, freqs) % detector))

    even_v = 2 * np.arange(quarter)
    odd_v = even_v + 1
    even_im = -wave(even_v, np.sin)
    even_im[:, 0] = np.where(place % 2 == 0, 1.0, -1.0)
    row_even = np.concatenate([wave(even_v, np.cos), even_im], axis=1)
    row_odd = np.concatenate([wave(odd_v, np.cos), -wave(odd_v, np.sin)], axis=1)
    row = np.stack([row_even, row_odd])

    even_u = 2 * np.arange(half)
    cols = []
    invs = []
    order = place.reshape(half // BLK, BLK // 2, 2).transpose(0, 2, 1).reshape(-1)
    for freqs in (even_u, even_u + 1):
        cos, sin = wave(freqs, np.cos), wave(freqs, np.sin)
        cols.append(np.concatenate([cos.T, sin.T], axis=0))
        invs.append(np.concatenate([cos[order], sin[order]], axis=1))
    fin = np.stack([row_even.T, row_odd.T]) / (detector * detector)

    keep = np.zeros((half, half))
    flip = np.zeros((half, half))
    for slot, freq in enumerate(np.concatenate([even_v, odd_v])):
        keep[freq, slot] = 1.0
        flip[(half - freq) % half, slot] = 1.0
    perm = np.stack([keep, flip]).astype(jnp.bfloat16)
    return halves(row), halves(np.stack(cols)), halves(np.stack(invs)), halves(fin), perm


def split(value):
    high = value.astype(BF16)
    return high, (value - high.astype(F32)).astype(BF16)


def dot(left, right):
    return jnp.dot(left, right, preferred_element_type=F32)


def dot3(left, right):
    return dot(left[0], right[0]) + dot(left[1], right[0]) + dot(left[0], right[1])


def prepare_kernel(rank_ref, out_ref):
    out_ref[...] = rank_ref[...]


def prepare(owner_rank):
    return pl.pallas_call(
        prepare_kernel,
        out_shape=jax.ShapeDtypeStruct(owner_rank.shape, jnp.int32),
        in_specs=[pl.BlockSpec(memory_space=VMEM)],
        out_specs=pl.BlockSpec(memory_space=VMEM),
        compiler_params=pltpu.CompilerParams(vmem_limit_bytes=16 << 20),
        cost_estimate=pl.CostEstimate(flops=PREPARE_COST, bytes_accessed=1024, transcendentals=0),
        name="prepare",
    )(owner_rank)


def pack_kernel(rank_ref, frames_ref, *outs):
    me = lax.axis_index("strip")
    ranks = rank_ref[...]
    places = lax.broadcasted_iota(jnp.int32, ranks.shape, 1)
    for j, out in enumerate(outs):
        out[...] = frames_ref[jnp.sum(jnp.where(ranks == (me ^ j), places, 0))]


def pack(owner_rank, frames):
    count, rows, detector = frames.shape
    return pl.pallas_call(
        pack_kernel,
        out_shape=[jax.ShapeDtypeStruct((rows, detector), F32)] * count,
        in_specs=[pl.BlockSpec(memory_space=VMEM)] * 2,
        out_specs=[pl.BlockSpec(memory_space=VMEM)] * count,
        compiler_params=pltpu.CompilerParams(vmem_limit_bytes=16 << 20),
        cost_estimate=pl.CostEstimate(flops=PACK_COST, bytes_accessed=1024, transcendentals=0),
        name="pack",
    )(owner_rank, frames)


def stack_kernel(*refs):
    for i, ref in enumerate(refs[:-1]):
        refs[-1][i] = ref[...]


def stack(parts):
    return pl.pallas_call(
        stack_kernel,
        out_shape=jax.ShapeDtypeStruct((len(parts),) + parts[0].shape, F32),
        in_specs=[pl.BlockSpec(memory_space=VMEM)] * len(parts),
        out_specs=pl.BlockSpec(memory_space=VMEM),
        compiler_params=pltpu.CompilerParams(vmem_limit_bytes=8 << 20),
        cost_estimate=pl.CostEstimate(flops=LITTLE, bytes_accessed=1024, transcendentals=0),
        name="stack",
    )(*parts)


def turned(left, right):
    return lax.dot_general(left, right, (((0,), (0,)), ((), ())), preferred_element_type=F32)


def fold_half(value, table, out_ref, which, tile):
    high, low = split(value)
    both = turned(high, table) + turned(low, table)
    for group in range(2):
        out_ref[which, group, pl.ds(pl.multiple_of(tile * 128, 128), 128)] = both[:, group * 128 : (group + 1) * 128]


def fold_pieces(quads, perm_ref, out_ref, held):
    strip, group = lax.axis_index("strip"), lax.axis_index("frames")
    for side in range(2):
        upper = (strip // 4) ^ side
        for t in range(4):
            base = pl.multiple_of(((strip ^ t) % 4) * BLK, BLK)
            held[side, t * BLK : (t + 1) * BLK] = perm_ref[upper, pl.ds(base, BLK)]
        for df in range(4):
            for part in range(2):
                value = jnp.concatenate([quads[2 * df + t % 2][2 * side + t // 2, part] for t in range(4)], axis=0)
                fold_half(value, held[side], out_ref, part + 2 * upper, group ^ df)


def fold_whole(kern, perm_ref, out_ref, held):
    half = perm_ref.shape[1]
    for side in range(2):
        for part in range(2):
            for tile in range(2 * half // 128):
                value = kern[0][part, side * half : (side + 1) * half, tile * 128 : (tile + 1) * 128]
                fold_half(value, perm_ref[side], out_ref, part + 2 * side, tile)


def rows_kernel(split_strip, lower_ref, upper_ref, row_ref, out_ref):
    rows, half = lower_ref.shape[0], lower_ref.shape[1] // 2
    one, two = lower_ref[...], upper_ref[...]
    diff = one - two
    if split_strip:
        diff = jnp.where(lax.axis_index("strip") >= split_strip, -diff, diff)
    both = jnp.concatenate([one + two, diff], axis=0)
    left, right = both[:, 0:half], both[:, half:]
    for group, value in enumerate((left + right, left - right)):
        parts = split(dot3(split(value), (row_ref[0, group], row_ref[1, group])))
        for i, part in enumerate(parts):
            for parity in range(2):
                out_ref[i, parity, :, group * half : (group + 1) * half] = part[parity * rows : (parity + 1) * rows]


def row_spectra(lower, upper, table, split_strip, flops):
    rows, detector = lower.shape
    return pl.pallas_call(
        functools.partial(rows_kernel, split_strip),
        out_shape=jax.ShapeDtypeStruct((2, 2, rows, detector), BF16),
        in_specs=[pl.BlockSpec(memory_space=VMEM)] * 3,
        out_specs=pl.BlockSpec(memory_space=VMEM),
        compiler_params=pltpu.CompilerParams(vmem_limit_bytes=16 << 20),
        cost_estimate=pl.CostEstimate(flops=flops, bytes_accessed=1024, transcendentals=0),
        name="rows",
    )(lower, upper, table)


def correlate_kernel(pieces, fold_body, *refs):
    (col_ref, inv_ref, fin_ref), lists, refs = refs[:3], refs[3:6], refs[6:]
    spectra, kern, perm_ref, out_ref = refs[:pieces], refs[pieces:-11], refs[-11], refs[-10]
    held, fold_ref, spec, img, blocks, *scalars, list_sems = refs[-9:]
    copies = [pltpu.make_async_copy(x, y, list_sems.at[i]) for i, (x, y) in enumerate(zip(lists, scalars))]
    for copy in copies:
        copy.start()
    fold_body(kern, perm_ref, fold_ref, held)
    detector = fold_ref.shape[2]
    half, quarter = detector // 2, detector // 4
    me = lax.axis_index("strip")
    rows = half // pieces
    for j in range(pieces):
        base = pl.multiple_of(((me ^ j) % pieces) * rows, rows)
        spec[:, :, pl.ds(base, rows)] = spectra[j][...]

    lane = lax.broadcasted_iota(jnp.int32, (half, quarter), 1)
    back = []
    for parity in range(2):
        table = (col_ref[0, parity], col_ref[1, parity])
        parts = []
        for group in range(2):
            lanes = slice(group * half, (group + 1) * half)
            both = dot3(table, (spec[0, parity, :, lanes], spec[1, parity, :, lanes]))
            cos_re, cos_im = both[0:half, 0:quarter], both[0:half, quarter:]
            sin_re, sin_im = both[half:, 0:quarter], both[half:, quarter:]
            freqs = pl.ds(parity, half, stride=2)
            up_re, up_im = fold_ref[0, group, freqs, :], fold_ref[1, group, freqs, :]
            dn_re, dn_im = fold_ref[2, group, freqs, :], fold_ref[3, group, freqs, :]
            a_re, a_im = cos_re + sin_im, cos_im - sin_re
            b_re, b_im = cos_re - sin_im, -cos_im - sin_re
            if group == 0:
                a_re, a_im = jnp.where(lane == 0, cos_re, a_re), jnp.where(lane == 0, -sin_re, a_im)
                b_re, b_im = jnp.where(lane == 0, cos_im, b_re), jnp.where(lane == 0, -sin_im, b_im)
            p_re, p_im = a_re * up_re - a_im * up_im, a_re * up_im + a_im * up_re
            q_re, q_im = b_re * dn_re - b_im * dn_im, b_re * dn_im + b_im * dn_re
            plus_re, minus_im = p_re + q_re, p_im - q_im
            less_im, minus_re = -p_im - q_im, p_re - q_re
            if group == 0:
                plus_re, minus_im = jnp.where(lane == 0, p_re, plus_re), jnp.where(lane == 0, q_re, minus_im)
                less_im, minus_re = jnp.where(lane == 0, -p_im, less_im), jnp.where(lane == 0, -q_im, minus_re)
            upper = split(jnp.concatenate([plus_re, minus_im], axis=1))
            lower = split(jnp.concatenate([less_im, minus_re], axis=1))
            parts.append([jnp.concatenate([u, w], axis=0) for u, w in zip(upper, lower)])
        table = (inv_ref[0, parity], inv_ref[1, parity])
        back.append([dot3(table, part) for part in parts])

    for upper in range(2):
        ends = []
        for group in range(2):
            even, odd = back[0][group], back[1][group]
            rows = split(even - odd if upper else even + odd)
            ends.append(dot3(rows, (fin_ref[0, group], fin_ref[1, group])))
        where = slice(upper * half, (upper + 1) * half)
        for side, value in enumerate((ends[0] + ends[1], ends[0] - ends[1])):
            for t in range(half // 128):
                img[side * (half // 128) + t, where] = value[:, t * 128 : (t + 1) * 128]

    for copy in copies:
        copy.wait()
    rank_ref, ids_ref, counts_ref = scalars
    own = jnp.int32(0)
    for i in range(rank_ref.shape[1]):
        own = own + jnp.where(rank_ref[0, i] == me, i, 0)
    used = counts_ref[own]
    pairs = BLK // 2
    lane = lax.broadcasted_iota(jnp.int32, (pairs, 2 * BLK), 1)
    for m in range(MAXB):
        block = jnp.clip(ids_ref[own, m], 0, NB * NB - 1)
        base = pl.multiple_of((block // NB) * BLK, BLK)
        tile = (block % NB) // 2
        even = img[tile, pl.ds(base, pairs)]
        odd = img[tile, pl.ds(base + pairs, pairs)]
        second = jnp.broadcast_to(block % 2 == 1, lane.shape)
        value = jnp.where(
            lane < BLK,
            jnp.where(second, pltpu.roll(even, BLK, 1), even),
            jnp.where(second, odd, pltpu.roll(odd, BLK, 1)),
        )
        blocks[m * pairs : (m + 1) * pairs] = jnp.where(m < used, value, 0.0)
    for j in range(pairs):
        out_ref[0, :, j * 2 * BLK : (j + 1) * 2 * BLK] = blocks[pl.ds(j, MAXB, stride=pairs), :]


def correlate(owner_rank, block_ids, block_counts, spectra, fold_body, kern, perm, consts):
    detector = spectra[0].shape[-1]
    half = detector // 2
    return pl.pallas_call(
        functools.partial(correlate_kernel, len(spectra), fold_body),
        out_shape=jax.ShapeDtypeStruct((1, MAXB, BLK * BLK), F32),
        in_specs=[pl.BlockSpec(memory_space=VMEM)] * 3
        + [pl.BlockSpec(memory_space=pl.ANY)] * 3
        + [pl.BlockSpec(memory_space=VMEM)] * (len(spectra) + len(kern) + 1),
        out_specs=pl.BlockSpec(memory_space=VMEM),
        scratch_shapes=[
            VMEM((2, half, half), BF16),
            VMEM((4, 2, detector, detector // 4), F32),
            VMEM((2, 2, half, detector), BF16),
            VMEM((detector // 128, detector, 128), F32),
            VMEM((MAXB * BLK // 2, 2 * BLK), F32),
        ]
        + [SMEM(x.shape, jnp.int32) for x in (owner_rank, block_ids, block_counts)]
        + [pltpu.SemaphoreType.DMA((3,))],
        compiler_params=pltpu.CompilerParams(vmem_limit_bytes=48 << 20),
        name="correlate",
    )(*consts, owner_rank, block_ids, block_counts, *spectra, *kern, perm)


def swap(value, axis, size, bits):
    return lax.ppermute(value, axis, [(i, i ^ bits) for i in range(size)])


def after(value, *others):
    return lax.optimization_barrier((value, others))[0]


def gather_and_spread(owner_rank, frames, kernel):
    piece = jnp.swapaxes(kernel, 1, 2)
    blocks = pack(prepare(owner_rank), frames)
    far = swap(piece, "strip", 8, 4)
    near = swap(piece, "strip", 8, 2)
    both = swap(far, "strip", 8, 2)
    quad = stack([piece, near, far, both])
    quad_x = swap(quad, "strip", 8, 1)
    quad_y = swap(quad, "frames", 4, 2)
    quad_xy = swap(quad_x, "frames", 4, 2)
    quads = [quad, quad_x, quad_y, quad_xy]
    sibling = [swap(after(quad, quad_x), "frames", 4, 1)]
    sibling += [swap(q, "frames", 4, 1) for q in quads[1:]]
    strips = [blocks[0]]
    for j in range(1, 8):
        strips.append(swap(after(blocks[j], quad_y) if j == 5 else blocks[j], "strip", 8, j))
    strips[0], strips[4] = after((strips[0], strips[4]), quad)
    return strips, [(sibling if df % 2 else quads)[2 * (df // 2) + dx] for df in range(4) for dx in range(2)]


def shards(strip_size, group_size, frames, kernel, owner_rank, block_ids, block_counts):
    detector = frames.shape[2]
    row_table, *consts, perm = tables(detector)
    if strip_size == 8 and group_size == 4:
        strips, kern = gather_and_spread(owner_rank, frames, kernel)
        spectra = [row_spectra(strips[j], strips[j + 4], row_table, 4, ROW_COSTS[j]) for j in range(4)]
        fold_body = fold_pieces
    else:
        places = jnp.argsort(owner_rank.reshape(-1))
        frame = lax.all_to_all(frames[places], "strip", split_axis=0, concat_axis=1, tiled=True)[0]
        whole = lax.all_gather(kernel, "strip", axis=2, tiled=True)
        whole = lax.all_gather(whole, "frames", axis=1, tiled=True)
        fold_body, kern = fold_whole, [jnp.swapaxes(whole, 1, 2)]
        spectra = [row_spectra(frame[: detector // 2], frame[detector // 2 :], row_table, 0, LITTLE)]
    return correlate(owner_rank, block_ids, block_counts, spectra, fold_body, kern, perm, consts)


def solution(mesh):
    return jax.shard_map(
        functools.partial(shards, mesh.shape["strip"], mesh.shape["frames"]),
        mesh=mesh,
        in_specs=(
            P("frames", "strip", None),
            P(None, "frames", "strip"),
            P("frames", None),
            P("frames", None),
            P("frames"),
        ),
        out_specs=P("strip", "frames", None),
        check_vma=False,
    )
```

```python
import functools

import jax
import jax.numpy as jnp
import numpy as np
from jax import lax
from jax.experimental import pallas as pl
from jax.experimental.pallas import tpu as pltpu
from jax.sharding import PartitionSpec as P

BLK = 64
NB = 8
MAXB = 16

VMEM = pltpu.VMEM
SMEM = pltpu.SMEM
BF16 = jnp.bfloat16

LITTLE = 1024
PREPARE_COST = 5_000_000_000
STACK_COST = 2_000_000_000
ROW_COSTS = (4_000_000_000, 6_000_000_000, 1_000_000_000, 1_500_000_000)
F32 = jnp.float32


def halves(table):
    high = table.astype(np.float32).astype(jnp.bfloat16)
    low = (table - high.astype(np.float64)).astype(np.float32).astype(jnp.bfloat16)
    return np.stack([high, low])


@functools.cache
def tables(detector):
    half = detector // 2
    quarter = detector // 4
    turn = 2.0 * np.pi / detector
    place = np.arange(half)

    def wave(freqs, function):
        return function(turn * (np.outer(place, freqs) % detector))

    even_v = 2 * np.arange(quarter)
    odd_v = even_v + 1
    even_im = -wave(even_v, np.sin)
    even_im[:, 0] = np.where(place % 2 == 0, 1.0, -1.0)
    row_even = np.concatenate([wave(even_v, np.cos), even_im], axis=1)
    row_odd = np.concatenate([wave(odd_v, np.cos), -wave(odd_v, np.sin)], axis=1)
    row = np.stack([row_even, row_odd])

    even_u = 2 * np.arange(half)
    cols = []
    invs = []
    order = place.reshape(half // BLK, BLK // 2, 2).transpose(0, 2, 1).reshape(-1)
    for freqs in (even_u, even_u + 1):
        cos, sin = wave(freqs, np.cos), wave(freqs, np.sin)
        cols.append(np.concatenate([cos.T, sin.T], axis=0))
        invs.append(np.concatenate([cos[order], sin[order]], axis=1))
    fin = np.stack([row_even.T, row_odd.T]) / (detector * detector)

    keep = np.zeros((half, half))
    flip = np.zeros((half, half))
    for slot, freq in enumerate(np.concatenate([even_v, odd_v])):
        keep[freq, slot] = 1.0
        flip[(half - freq) % half, slot] = 1.0
    perm = np.stack([keep, flip]).astype(jnp.bfloat16)
    return halves(row), halves(np.stack(cols)), halves(np.stack(invs)), halves(fin), perm


def split(value):
    high = value.astype(BF16)
    return high, (value - high.astype(F32)).astype(BF16)


def dot(left, right):
    return jnp.dot(left, right, preferred_element_type=F32)


def dot3(left, right):
    return dot(left[0], right[0]) + dot(left[1], right[0]) + dot(left[0], right[1])


def prepare_kernel(rank_ref, out_ref):
    out_ref[...] = rank_ref[...]


def prepare(owner_rank):
    return pl.pallas_call(
        prepare_kernel,
        out_shape=jax.ShapeDtypeStruct(owner_rank.shape, jnp.int32),
        in_specs=[pl.BlockSpec(memory_space=VMEM)],
        out_specs=pl.BlockSpec(memory_space=VMEM),
        compiler_params=pltpu.CompilerParams(vmem_limit_bytes=16 << 20),
        cost_estimate=pl.CostEstimate(flops=PREPARE_COST, bytes_accessed=1024, transcendentals=0),
        name="prepare",
    )(owner_rank)


def pack_kernel(rank_ref, frames_ref, *outs):
    me = lax.axis_index("strip")
    ranks = rank_ref[...]
    places = lax.broadcasted_iota(jnp.int32, ranks.shape, 1)
    for j, out in enumerate(outs):
        out[...] = frames_ref[jnp.sum(jnp.where(ranks == (me ^ j), places, 0))]


def pack(owner_rank, frames):
    count, rows, detector = frames.shape
    return pl.pallas_call(
        pack_kernel,
        out_shape=[jax.ShapeDtypeStruct((rows, detector), F32)] * count,
        in_specs=[pl.BlockSpec(memory_space=VMEM)] * 2,
        out_specs=[pl.BlockSpec(memory_space=VMEM)] * count,
        compiler_params=pltpu.CompilerParams(vmem_limit_bytes=16 << 20),
        cost_estimate=pl.CostEstimate(flops=LITTLE, bytes_accessed=1024, transcendentals=0),
        name="pack",
    )(owner_rank, frames)


def stack_kernel(*refs):
    for i, ref in enumerate(refs[:-1]):
        refs[-1][i] = ref[...]


def stack(parts):
    return pl.pallas_call(
        stack_kernel,
        out_shape=jax.ShapeDtypeStruct((len(parts),) + parts[0].shape, F32),
        in_specs=[pl.BlockSpec(memory_space=VMEM)] * len(parts),
        out_specs=pl.BlockSpec(memory_space=VMEM),
        compiler_params=pltpu.CompilerParams(vmem_limit_bytes=8 << 20),
        cost_estimate=pl.CostEstimate(flops=STACK_COST, bytes_accessed=1024, transcendentals=0),
        name="stack",
    )(*parts)


def turned(left, right):
    return lax.dot_general(left, right, (((0,), (0,)), ((), ())), preferred_element_type=F32)


def fold_half(value, table, out_ref, which, tile):
    high, low = split(value)
    both = turned(high, table) + turned(low, table)
    for group in range(2):
        out_ref[which, group, pl.ds(pl.multiple_of(tile * 128, 128), 128)] = both[:, group * 128 : (group + 1) * 128]


def fold_pieces(quads, perm_ref, out_ref, held):
    strip, group = lax.axis_index("strip"), lax.axis_index("frames")
    for side in range(2):
        upper = (strip // 4) ^ side
        for t in range(4):
            base = pl.multiple_of(((strip ^ t) % 4) * BLK, BLK)
            held[side, t * BLK : (t + 1) * BLK] = perm_ref[upper, pl.ds(base, BLK)]
        for df in range(4):
            for part in range(2):
                value = jnp.concatenate([quads[2 * df + t % 2][2 * side + t // 2, part] for t in range(4)], axis=0)
                fold_half(value, held[side], out_ref, part + 2 * upper, group ^ df)


def fold_whole(kern, perm_ref, out_ref, held):
    half = perm_ref.shape[1]
    for side in range(2):
        for part in range(2):
            for tile in range(2 * half // 128):
                value = kern[0][part, side * half : (side + 1) * half, tile * 128 : (tile + 1) * 128]
                fold_half(value, perm_ref[side], out_ref, part + 2 * side, tile)


def rows_kernel(split_strip, lower_ref, upper_ref, row_ref, out_ref):
    rows, half = lower_ref.shape[0], lower_ref.shape[1] // 2
    one, two = lower_ref[...], upper_ref[...]
    diff = one - two
    if split_strip:
        diff = jnp.where(lax.axis_index("strip") >= split_strip, -diff, diff)
    both = jnp.concatenate([one + two, diff], axis=0)
    left, right = both[:, 0:half], both[:, half:]
    for group, value in enumerate((left + right, left - right)):
        parts = split(dot3(split(value), (row_ref[0, group], row_ref[1, group])))
        for i, part in enumerate(parts):
            for parity in range(2):
                out_ref[i, parity, :, group * half : (group + 1) * half] = part[parity * rows : (parity + 1) * rows]


def row_spectra(lower, upper, table, split_strip, flops):
    rows, detector = lower.shape
    return pl.pallas_call(
        functools.partial(rows_kernel, split_strip),
        out_shape=jax.ShapeDtypeStruct((2, 2, rows, detector), BF16),
        in_specs=[pl.BlockSpec(memory_space=VMEM)] * 3,
        out_specs=pl.BlockSpec(memory_space=VMEM),
        compiler_params=pltpu.CompilerParams(vmem_limit_bytes=16 << 20),
        cost_estimate=pl.CostEstimate(flops=flops, bytes_accessed=1024, transcendentals=0),
        name="rows",
    )(lower, upper, table)


def correlate_kernel(pieces, fold_body, *refs):
    (col_ref, inv_ref, fin_ref), lists, refs = refs[:3], refs[3:6], refs[6:]
    spectra, kern, perm_ref, out_ref = refs[:pieces], refs[pieces:-11], refs[-11], refs[-10]
    held, fold_ref, spec, img, blocks, *scalars, list_sems = refs[-9:]
    copies = [pltpu.make_async_copy(x, y, list_sems.at[i]) for i, (x, y) in enumerate(zip(lists, scalars))]
    for copy in copies:
        copy.start()
    fold_body(kern, perm_ref, fold_ref, held)
    detector = fold_ref.shape[2]
    half, quarter = detector // 2, detector // 4
    me = lax.axis_index("strip")
    rows = half // pieces
    for j in range(pieces):
        base = pl.multiple_of(((me ^ j) % pieces) * rows, rows)
        spec[:, :, pl.ds(base, rows)] = spectra[j][...]

    lane = lax.broadcasted_iota(jnp.int32, (half, quarter), 1)
    back = []
    for parity in range(2):
        table = (col_ref[0, parity], col_ref[1, parity])
        parts = []
        for group in range(2):
            lanes = slice(group * half, (group + 1) * half)
            both = dot3(table, (spec[0, parity, :, lanes], spec[1, parity, :, lanes]))
            cos_re, cos_im = both[0:half, 0:quarter], both[0:half, quarter:]
            sin_re, sin_im = both[half:, 0:quarter], both[half:, quarter:]
            freqs = pl.ds(parity, half, stride=2)
            up_re, up_im = fold_ref[0, group, freqs, :], fold_ref[1, group, freqs, :]
            dn_re, dn_im = fold_ref[2, group, freqs, :], fold_ref[3, group, freqs, :]
            a_re, a_im = cos_re + sin_im, cos_im - sin_re
            b_re, b_im = cos_re - sin_im, -cos_im - sin_re
            if group == 0:
                a_re, a_im = jnp.where(lane == 0, cos_re, a_re), jnp.where(lane == 0, -sin_re, a_im)
                b_re, b_im = jnp.where(lane == 0, cos_im, b_re), jnp.where(lane == 0, -sin_im, b_im)
            p_re, p_im = a_re * up_re - a_im * up_im, a_re * up_im + a_im * up_re
            q_re, q_im = b_re * dn_re - b_im * dn_im, b_re * dn_im + b_im * dn_re
            plus_re, minus_im = p_re + q_re, p_im - q_im
            less_im, minus_re = -p_im - q_im, p_re - q_re
            if group == 0:
                plus_re, minus_im = jnp.where(lane == 0, p_re, plus_re), jnp.where(lane == 0, q_re, minus_im)
                less_im, minus_re = jnp.where(lane == 0, -p_im, less_im), jnp.where(lane == 0, -q_im, minus_re)
            upper = split(jnp.concatenate([plus_re, minus_im], axis=1))
            lower = split(jnp.concatenate([less_im, minus_re], axis=1))
            parts.append([jnp.concatenate([u, w], axis=0) for u, w in zip(upper, lower)])
        table = (inv_ref[0, parity], inv_ref[1, parity])
        back.append([dot3(table, part) for part in parts])

    for upper in range(2):
        ends = []
        for group in range(2):
            even, odd = back[0][group], back[1][group]
            rows = split(even - odd if upper else even + odd)
            ends.append(dot3(rows, (fin_ref[0, group], fin_ref[1, group])))
        where = slice(upper * half, (upper + 1) * half)
        for side, value in enumerate((ends[0] + ends[1], ends[0] - ends[1])):
            for t in range(half // 128):
                img[side * (half // 128) + t, where] = value[:, t * 128 : (t + 1) * 128]

    for copy in copies:
        copy.wait()
    rank_ref, ids_ref, counts_ref = scalars
    own = jnp.int32(0)
    for i in range(rank_ref.shape[1]):
        own = own + jnp.where(rank_ref[0, i] == me, i, 0)
    used = counts_ref[own]
    pairs = BLK // 2
    lane = lax.broadcasted_iota(jnp.int32, (pairs, 2 * BLK), 1)
    for m in range(MAXB):
        block = jnp.clip(ids_ref[own, m], 0, NB * NB - 1)
        base = pl.multiple_of((block // NB) * BLK, BLK)
        tile = (block % NB) // 2
        even = img[tile, pl.ds(base, pairs)]
        odd = img[tile, pl.ds(base + pairs, pairs)]
        second = jnp.broadcast_to(block % 2 == 1, lane.shape)
        value = jnp.where(
            lane < BLK,
            jnp.where(second, pltpu.roll(even, BLK, 1), even),
            jnp.where(second, odd, pltpu.roll(odd, BLK, 1)),
        )
        blocks[m * pairs : (m + 1) * pairs] = jnp.where(m < used, value, 0.0)
    for j in range(pairs):
        out_ref[0, :, j * 2 * BLK : (j + 1) * 2 * BLK] = blocks[pl.ds(j, MAXB, stride=pairs), :]


def correlate(owner_rank, block_ids, block_counts, spectra, fold_body, kern, perm, consts):
    detector = spectra[0].shape[-1]
    half = detector // 2
    return pl.pallas_call(
        functools.partial(correlate_kernel, len(spectra), fold_body),
        out_shape=jax.ShapeDtypeStruct((1, MAXB, BLK * BLK), F32),
        in_specs=[pl.BlockSpec(memory_space=VMEM)] * 3
        + [pl.BlockSpec(memory_space=pl.ANY)] * 3
        + [pl.BlockSpec(memory_space=VMEM)] * (len(spectra) + len(kern) + 1),
        out_specs=pl.BlockSpec(memory_space=VMEM),
        scratch_shapes=[
            VMEM((2, half, half), BF16),
            VMEM((4, 2, detector, detector // 4), F32),
            VMEM((2, 2, half, detector), BF16),
            VMEM((detector // 128, detector, 128), F32),
            VMEM((MAXB * BLK // 2, 2 * BLK), F32),
        ]
        + [SMEM(x.shape, jnp.int32) for x in (owner_rank, block_ids, block_counts)]
        + [pltpu.SemaphoreType.DMA((3,))],
        compiler_params=pltpu.CompilerParams(vmem_limit_bytes=48 << 20),
        name="correlate",
    )(*consts, owner_rank, block_ids, block_counts, *spectra, *kern, perm)


def swap(value, axis, size, bits):
    return lax.ppermute(value, axis, [(i, i ^ bits) for i in range(size)])


def after(value, *others):
    return lax.optimization_barrier((value, others))[0]


def gather_and_spread(owner_rank, frames, kernel):
    piece = jnp.swapaxes(kernel, 1, 2)
    blocks = pack(prepare(owner_rank), frames)
    strips = [blocks[0]] + [None] * 7

    def send(j, *others):
        strips[j] = swap(after(blocks[j], *others) if others else blocks[j], "strip", 8, j)

    far = swap(piece, "strip", 8, 4)
    near = swap(piece, "strip", 8, 2)
    across = swap(piece, "strip", 8, 6)
    quad = stack([piece, near, far, across])
    quad_x = swap(quad, "strip", 8, 1)
    send(7)
    quad_y = swap(after(quad, strips[7]), "frames", 4, 2)
    quad_xy = swap(quad_x, "frames", 4, 2)
    quads = [quad, quad_x, quad_y, quad_xy]
    sibling = [swap(after(quad, quad_x), "frames", 4, 1)]
    sibling += [swap(q, "frames", 4, 1) for q in quads[1:]]
    send(1)
    send(2)
    send(3)
    send(4, far)
    send(5, quad_y)
    send(6)
    return strips, [(sibling if df % 2 else quads)[2 * (df // 2) + dx] for df in range(4) for dx in range(2)]


def shards(strip_size, group_size, frames, kernel, owner_rank, block_ids, block_counts):
    detector = frames.shape[2]
    row_table, *consts, perm = tables(detector)
    if strip_size == 8 and group_size == 4:
        strips, kern = gather_and_spread(owner_rank, frames, kernel)
        spectra = [row_spectra(strips[j], strips[j + 4], row_table, 4, ROW_COSTS[j]) for j in range(4)]
        fold_body = fold_pieces
    else:
        places = jnp.argsort(owner_rank.reshape(-1))
        frame = lax.all_to_all(frames[places], "strip", split_axis=0, concat_axis=1, tiled=True)[0]
        whole = lax.all_gather(kernel, "strip", axis=2, tiled=True)
        whole = lax.all_gather(whole, "frames", axis=1, tiled=True)
        fold_body, kern = fold_whole, [jnp.swapaxes(whole, 1, 2)]
        spectra = [row_spectra(frame[: detector // 2], frame[detector // 2 :], row_table, 0, LITTLE)]
    return correlate(owner_rank, block_ids, block_counts, spectra, fold_body, kern, perm, consts)


def solution(mesh):
    return jax.shard_map(
        functools.partial(shards, mesh.shape["strip"], mesh.shape["frames"]),
        mesh=mesh,
        in_specs=(
            P("frames", "strip", None),
            P(None, "frames", "strip"),
            P("frames", None),
            P("frames", None),
            P("frames"),
        ),
        out_specs=P("strip", "frames", None),
        check_vma=False,
    )
```

```python
import functools

import jax
import jax.numpy as jnp
import numpy as np
from jax import lax
from jax.experimental import pallas as pl
from jax.experimental.pallas import tpu as pltpu
from jax.sharding import PartitionSpec as P

BLK = 64
NB = 8
MAXB = 16

VMEM = pltpu.VMEM
SMEM = pltpu.SMEM
BF16 = jnp.bfloat16

LITTLE = 1024
PREPARE_COST = 5_000_000_000
STACK_COST = 2_000_000_000
ROW_COSTS = (4_000_000_000, 6_000_000_000, 1_000_000_000, 1_500_000_000)
F32 = jnp.float32


def halves(table):
    high = table.astype(np.float32).astype(jnp.bfloat16)
    low = (table - high.astype(np.float64)).astype(np.float32).astype(jnp.bfloat16)
    return np.stack([high, low])


@functools.cache
def tables(detector):
    half = detector // 2
    quarter = detector // 4
    turn = 2.0 * np.pi / detector
    place = np.arange(half)

    def wave(freqs, function):
        return function(turn * (np.outer(place, freqs) % detector))

    even_v = 2 * np.arange(quarter)
    odd_v = even_v + 1
    even_im = -wave(even_v, np.sin)
    even_im[:, 0] = np.where(place % 2 == 0, 1.0, -1.0)
    row_even = np.concatenate([wave(even_v, np.cos), even_im], axis=1)
    row_odd = np.concatenate([wave(odd_v, np.cos), -wave(odd_v, np.sin)], axis=1)
    row = np.stack([row_even, row_odd])

    even_u = 2 * np.arange(half)
    cols = []
    invs = []
    order = place.reshape(half // BLK, BLK // 2, 2).transpose(0, 2, 1).reshape(-1)
    for freqs in (even_u, even_u + 1):
        cos, sin = wave(freqs, np.cos), wave(freqs, np.sin)
        cols.append(np.concatenate([cos.T, sin.T], axis=0))
        invs.append(np.concatenate([cos[order], sin[order]], axis=1))
    fin = np.stack([row_even.T, row_odd.T]) / (detector * detector)

    keep = np.zeros((half, half))
    flip = np.zeros((half, half))
    for slot, freq in enumerate(np.concatenate([even_v, odd_v])):
        keep[freq, slot] = 1.0
        flip[(half - freq) % half, slot] = 1.0
    perm = np.stack([keep, flip]).astype(jnp.bfloat16)
    return halves(row), halves(np.stack(cols)), halves(np.stack(invs)), halves(fin), perm


def split(value):
    high = value.astype(BF16)
    return high, (value - high.astype(F32)).astype(BF16)


def dot(left, right):
    return jnp.dot(left, right, preferred_element_type=F32)


def dot3(left, right):
    return dot(left[0], right[0]) + dot(left[1], right[0]) + dot(left[0], right[1])


def prepare_kernel(rank_ref, out_ref):
    out_ref[...] = rank_ref[...]


def prepare(owner_rank):
    return pl.pallas_call(
        prepare_kernel,
        out_shape=jax.ShapeDtypeStruct(owner_rank.shape, jnp.int32),
        in_specs=[pl.BlockSpec(memory_space=VMEM)],
        out_specs=pl.BlockSpec(memory_space=VMEM),
        compiler_params=pltpu.CompilerParams(vmem_limit_bytes=16 << 20),
        cost_estimate=pl.CostEstimate(flops=PREPARE_COST, bytes_accessed=1024, transcendentals=0),
        name="prepare",
    )(owner_rank)


def pack_kernel(rank_ref, frames_ref, *outs):
    me = lax.axis_index("strip")
    ranks = rank_ref[...]
    places = lax.broadcasted_iota(jnp.int32, ranks.shape, 1)
    for j, out in enumerate(outs):
        out[...] = frames_ref[jnp.sum(jnp.where(ranks == (me ^ j), places, 0))]


def pack(owner_rank, frames):
    count, rows, detector = frames.shape
    return pl.pallas_call(
        pack_kernel,
        out_shape=[jax.ShapeDtypeStruct((rows, detector), F32)] * count,
        in_specs=[pl.BlockSpec(memory_space=VMEM)] * 2,
        out_specs=[pl.BlockSpec(memory_space=VMEM)] * count,
        compiler_params=pltpu.CompilerParams(vmem_limit_bytes=16 << 20),
        cost_estimate=pl.CostEstimate(flops=LITTLE, bytes_accessed=1024, transcendentals=0),
        name="pack",
    )(owner_rank, frames)


def stack_kernel(*refs):
    for i, ref in enumerate(refs[:-1]):
        refs[-1][i] = ref[...]


def stack(parts):
    return pl.pallas_call(
        stack_kernel,
        out_shape=jax.ShapeDtypeStruct((len(parts),) + parts[0].shape, F32),
        in_specs=[pl.BlockSpec(memory_space=VMEM)] * len(parts),
        out_specs=pl.BlockSpec(memory_space=VMEM),
        compiler_params=pltpu.CompilerParams(vmem_limit_bytes=8 << 20),
        cost_estimate=pl.CostEstimate(flops=STACK_COST, bytes_accessed=1024, transcendentals=0),
        name="stack",
    )(*parts)


def turned(left, right):
    return lax.dot_general(left, right, (((0,), (0,)), ((), ())), preferred_element_type=F32)


def fold_half(value, table, out_ref, which, tile):
    high, low = split(value)
    both = turned(high, table) + turned(low, table)
    for group in range(2):
        out_ref[which, group, pl.ds(pl.multiple_of(tile * 128, 128), 128)] = both[:, group * 128 : (group + 1) * 128]


def fold_pieces(quads, perm_ref, out_ref, held):
    strip, group = lax.axis_index("strip"), lax.axis_index("frames")
    for side in range(2):
        upper = (strip // 4) ^ side
        for t in range(4):
            base = pl.multiple_of(((strip ^ t) % 4) * BLK, BLK)
            held[side, t * BLK : (t + 1) * BLK] = perm_ref[upper, pl.ds(base, BLK)]
        for df in range(4):
            for part in range(2):
                value = jnp.concatenate([quads[2 * df + t % 2][2 * side + t // 2, part] for t in range(4)], axis=0)
                fold_half(value, held[side], out_ref, part + 2 * upper, group ^ df)


def fold_whole(kern, perm_ref, out_ref, held):
    half = perm_ref.shape[1]
    for side in range(2):
        for part in range(2):
            for tile in range(2 * half // 128):
                value = kern[0][part, side * half : (side + 1) * half, tile * 128 : (tile + 1) * 128]
                fold_half(value, perm_ref[side], out_ref, part + 2 * side, tile)


def rows_kernel(split_strip, lower_ref, upper_ref, row_ref, out_ref):
    rows, half = lower_ref.shape[0], lower_ref.shape[1] // 2
    one, two = lower_ref[...], upper_ref[...]
    diff = one - two
    if split_strip:
        diff = jnp.where(lax.axis_index("strip") >= split_strip, -diff, diff)
    both = jnp.concatenate([one + two, diff], axis=0)
    left, right = both[:, 0:half], both[:, half:]
    for group, value in enumerate((left + right, left - right)):
        parts = split(dot3(split(value), (row_ref[0, group], row_ref[1, group])))
        for i, part in enumerate(parts):
            for parity in range(2):
                out_ref[i, parity, :, group * half : (group + 1) * half] = part[parity * rows : (parity + 1) * rows]


def row_spectra(lower, upper, table, split_strip, flops):
    rows, detector = lower.shape
    return pl.pallas_call(
        functools.partial(rows_kernel, split_strip),
        out_shape=jax.ShapeDtypeStruct((2, 2, rows, detector), BF16),
        in_specs=[pl.BlockSpec(memory_space=VMEM)] * 3,
        out_specs=pl.BlockSpec(memory_space=VMEM),
        compiler_params=pltpu.CompilerParams(vmem_limit_bytes=16 << 20),
        cost_estimate=pl.CostEstimate(flops=flops, bytes_accessed=1024, transcendentals=0),
        name="rows",
    )(lower, upper, table)


def correlate_kernel(pieces, fold_body, *refs):
    (col_ref, inv_ref, fin_ref), lists, refs = refs[:3], refs[3:6], refs[6:]
    spectra, kern, perm_ref, out_ref = refs[:pieces], refs[pieces:-11], refs[-11], refs[-10]
    held, fold_ref, spec, img, blocks, *scalars, list_sems = refs[-9:]
    copies = [pltpu.make_async_copy(x, y, list_sems.at[i]) for i, (x, y) in enumerate(zip(lists, scalars))]
    for copy in copies:
        copy.start()
    fold_body(kern, perm_ref, fold_ref, held)
    detector = fold_ref.shape[2]
    half, quarter = detector // 2, detector // 4
    me = lax.axis_index("strip")
    rows = half // pieces
    for j in range(pieces):
        base = pl.multiple_of(((me ^ j) % pieces) * rows, rows)
        spec[:, :, pl.ds(base, rows)] = spectra[j][...]

    lane = lax.broadcasted_iota(jnp.int32, (half, quarter), 1)
    back = []
    for parity in range(2):
        table = (col_ref[0, parity], col_ref[1, parity])
        parts = []
        for group in range(2):
            lanes = slice(group * half, (group + 1) * half)
            both = dot3(table, (spec[0, parity, :, lanes], spec[1, parity, :, lanes]))
            cos_re, cos_im = both[0:half, 0:quarter], both[0:half, quarter:]
            sin_re, sin_im = both[half:, 0:quarter], both[half:, quarter:]
            freqs = pl.ds(parity, half, stride=2)
            up_re, up_im = fold_ref[0, group, freqs, :], fold_ref[1, group, freqs, :]
            dn_re, dn_im = fold_ref[2, group, freqs, :], fold_ref[3, group, freqs, :]
            a_re, a_im = cos_re + sin_im, cos_im - sin_re
            b_re, b_im = cos_re - sin_im, -cos_im - sin_re
            if group == 0:
                a_re, a_im = jnp.where(lane == 0, cos_re, a_re), jnp.where(lane == 0, -sin_re, a_im)
                b_re, b_im = jnp.where(lane == 0, cos_im, b_re), jnp.where(lane == 0, -sin_im, b_im)
            p_re, p_im = a_re * up_re - a_im * up_im, a_re * up_im + a_im * up_re
            q_re, q_im = b_re * dn_re - b_im * dn_im, b_re * dn_im + b_im * dn_re
            plus_re, minus_im = p_re + q_re, p_im - q_im
            less_im, minus_re = -p_im - q_im, p_re - q_re
            if group == 0:
                plus_re, minus_im = jnp.where(lane == 0, p_re, plus_re), jnp.where(lane == 0, q_re, minus_im)
                less_im, minus_re = jnp.where(lane == 0, -p_im, less_im), jnp.where(lane == 0, -q_im, minus_re)
            upper = split(jnp.concatenate([plus_re, minus_im], axis=1))
            lower = split(jnp.concatenate([less_im, minus_re], axis=1))
            parts.append([jnp.concatenate([u, w], axis=0) for u, w in zip(upper, lower)])
        table = (inv_ref[0, parity], inv_ref[1, parity])
        back.append([dot3(table, part) for part in parts])

    for upper in range(2):
        ends = []
        for group in range(2):
            even, odd = back[0][group], back[1][group]
            rows = split(even - odd if upper else even + odd)
            ends.append(dot3(rows, (fin_ref[0, group], fin_ref[1, group])))
        where = slice(upper * half, (upper + 1) * half)
        for side, value in enumerate((ends[0] + ends[1], ends[0] - ends[1])):
            for t in range(half // 128):
                img[side * (half // 128) + t, where] = value[:, t * 128 : (t + 1) * 128]

    for copy in copies:
        copy.wait()
    rank_ref, ids_ref, counts_ref = scalars
    own = jnp.int32(0)
    for i in range(rank_ref.shape[1]):
        own = own + jnp.where(rank_ref[0, i] == me, i, 0)
    used = counts_ref[own]
    pairs = BLK // 2
    lane = lax.broadcasted_iota(jnp.int32, (pairs, 2 * BLK), 1)
    for m in range(MAXB):
        block = jnp.clip(ids_ref[own, m], 0, NB * NB - 1)
        base = pl.multiple_of((block // NB) * BLK, BLK)
        tile = (block % NB) // 2
        even = img[tile, pl.ds(base, pairs)]
        odd = img[tile, pl.ds(base + pairs, pairs)]
        second = jnp.broadcast_to(block % 2 == 1, lane.shape)
        value = jnp.where(
            lane < BLK,
            jnp.where(second, pltpu.roll(even, BLK, 1), even),
            jnp.where(second, odd, pltpu.roll(odd, BLK, 1)),
        )
        blocks[m * pairs : (m + 1) * pairs] = jnp.where(m < used, value, 0.0)
    for j in range(pairs):
        out_ref[0, :, j * 2 * BLK : (j + 1) * 2 * BLK] = blocks[pl.ds(j, MAXB, stride=pairs), :]


def correlate(owner_rank, block_ids, block_counts, spectra, fold_body, kern, perm, consts):
    detector = spectra[0].shape[-1]
    half = detector // 2
    return pl.pallas_call(
        functools.partial(correlate_kernel, len(spectra), fold_body),
        out_shape=jax.ShapeDtypeStruct((1, MAXB, BLK * BLK), F32),
        in_specs=[pl.BlockSpec(memory_space=VMEM)] * 3
        + [pl.BlockSpec(memory_space=pl.ANY)] * 3
        + [pl.BlockSpec(memory_space=VMEM)] * (len(spectra) + len(kern) + 1),
        out_specs=pl.BlockSpec(memory_space=VMEM),
        scratch_shapes=[
            VMEM((2, half, half), BF16),
            VMEM((4, 2, detector, detector // 4), F32),
            VMEM((2, 2, half, detector), BF16),
            VMEM((detector // 128, detector, 128), F32),
            VMEM((MAXB * BLK // 2, 2 * BLK), F32),
        ]
        + [SMEM(x.shape, jnp.int32) for x in (owner_rank, block_ids, block_counts)]
        + [pltpu.SemaphoreType.DMA((3,))],
        compiler_params=pltpu.CompilerParams(vmem_limit_bytes=48 << 20),
        name="correlate",
    )(*consts, owner_rank, block_ids, block_counts, *spectra, *kern, perm)


def swap(value, axis, size, bits):
    return lax.ppermute(value, axis, [(i, i ^ bits) for i in range(size)])


def after(value, *others):
    return lax.optimization_barrier((value, others))[0]


def gather_and_spread(owner_rank, frames, kernel):
    piece = jnp.swapaxes(kernel, 1, 2)
    blocks = pack(prepare(owner_rank), frames)
    strips = [blocks[0]] + [None] * 7

    def send(j, *others):
        strips[j] = swap(after(blocks[j], *others) if others else blocks[j], "strip", 8, j)

    far = swap(piece, "strip", 8, 4)
    near = swap(piece, "strip", 8, 2)
    across = swap(piece, "strip", 8, 6)
    quad = stack([piece, near, far, across])
    quad_x = swap(quad, "strip", 8, 1)
    send(7)
    quad_y = swap(after(quad, strips[7]), "frames", 4, 2)
    quad_xy = swap(quad_x, "frames", 4, 2)
    quads = [quad, quad_x, quad_y, quad_xy]
    sibling = [swap(after(quad, quad_x), "frames", 4, 1)]
    sibling += [swap(q, "frames", 4, 1) for q in quads[1:]]
    send(1)
    send(2)
    send(3, far)
    send(4, far)
    send(5, quad_y)
    send(6)
    return strips, [(sibling if df % 2 else quads)[2 * (df // 2) + dx] for df in range(4) for dx in range(2)]


def shards(strip_size, group_size, frames, kernel, owner_rank, block_ids, block_counts):
    detector = frames.shape[2]
    row_table, *consts, perm = tables(detector)
    if strip_size == 8 and group_size == 4:
        strips, kern = gather_and_spread(owner_rank, frames, kernel)
        spectra = [row_spectra(strips[j], strips[j + 4], row_table, 4, ROW_COSTS[j]) for j in range(4)]
        fold_body = fold_pieces
    else:
        places = jnp.argsort(owner_rank.reshape(-1))
        frame = lax.all_to_all(frames[places], "strip", split_axis=0, concat_axis=1, tiled=True)[0]
        whole = lax.all_gather(kernel, "strip", axis=2, tiled=True)
        whole = lax.all_gather(whole, "frames", axis=1, tiled=True)
        fold_body, kern = fold_whole, [jnp.swapaxes(whole, 1, 2)]
        spectra = [row_spectra(frame[: detector // 2], frame[detector // 2 :], row_table, 0, LITTLE)]
    return correlate(owner_rank, block_ids, block_counts, spectra, fold_body, kern, perm, consts)


def solution(mesh):
    return jax.shard_map(
        functools.partial(shards, mesh.shape["strip"], mesh.shape["frames"]),
        mesh=mesh,
        in_specs=(
            P("frames", "strip", None),
            P(None, "frames", "strip"),
            P("frames", None),
            P("frames", None),
            P("frames"),
        ),
        out_specs=P("strip", "frames", None),
        check_vma=False,
    )
```
